256 devices in a mesh: ctx: 16 (over y_hi, z), dp: 16 (over y_lo, x, core).
Axes of the slice: x: 4, y: 4 (y_hi: 2, y_lo: 2; y = y_hi * 2 + y_lo), z: 8, core: 2. Of those that a mesh axis runs over, the one named last changes fastest.
Arguments:
- inputs: bfloat16 [16, 3072, 8192], P('dp', 'ctx'), may hold values from -6 to 6
- query_saved: bfloat16 [16, 3072, 4096], P('dp', 'ctx'), may hold values from -17 to 17
- key_saved: bfloat16 [16, 3072, 512], P('dp', 'ctx'), may hold values from -17 to 17
- value_saved: bfloat16 [16, 3072, 512], P('dp', 'ctx'), may hold values from -6 to 6
- grad_out: bfloat16 [16, 3072, 4096], P('dp', 'ctx'), may hold values from -6 to 6
- value_weight: bfloat16 [8192, 512], P('dp'), may hold values from -6 to 6
- query_down_weight: bfloat16 [16, 8192], replicated, may hold values from -1.5 to 1.5
- up_q: bfloat16 [16, 4096], replicated, may hold values from -4 to 4
- value_down_weight: bfloat16 [16, 8192], replicated, may hold values from -1.5 to 1.5
- up_v: bfloat16 [16, 512], replicated, may hold values from -0.25 to 0.25
Outputs:
- grad_down_q: float32 [16, 8192], P(None, 'dp')
- grad_up_q: float32 [16, 4096], P(None, 'dp')
- grad_down_v: float32 [16, 8192], P(None, 'dp')
- grad_up_v: float32 [16, 512], P(None, 'dp')
- input_gradient: bfloat16 [16, 3072, 8192], P('dp', 'ctx')
The draws below stay inside these ranges and needn't reach their ends.
All inputs are finite; a program needn't handle non-finite values.
Results may differ from the reference program's by a relative error of at most 0.012.
Values may be sent and summed in bfloat16 or wider, within the bound.
A program may use at most 128 MiB of HBM per device.

```python
import math
import jax
import jax.numpy as jnp
from jax import lax

MODEL_WIDTH = 8192
HEAD_WIDTH = 128
LOCAL_Q_HEADS = 32
LOCAL_KV_HEADS = 4
R = 16
TOK_DEV = 192
DQ = 4096
DKV = 512
GROUP = 768
SEQUENCE_LENGTH = 3072
BATCH_SEQUENCES = 16


def shared_base(key):
    return jnp.clip(jax.random.normal(key, (BATCH_SEQUENCES, SEQUENCE_LENGTH, LOCAL_KV_HEADS, HEAD_WIDTH), jnp.float32), -3.0, 3.0)


def draw_key_saved(key, part):
    base = shared_base(key)
    keys_out = base
    return keys_out.reshape(BATCH_SEQUENCES, SEQUENCE_LENGTH, DKV).astype(jnp.bfloat16)


def draw_query_saved(key, part):
    key = jax.random.fold_in(key, 13)
    local_rows = jnp.clip(jax.random.normal(key, (BATCH_SEQUENCES, SEQUENCE_LENGTH, LOCAL_KV_HEADS, LOCAL_Q_HEADS // LOCAL_KV_HEADS, HEAD_WIDTH), jnp.float32), -3.0, 3.0)
    query_rows = local_rows
    return query_rows.reshape(BATCH_SEQUENCES, SEQUENCE_LENGTH, DQ).astype(jnp.bfloat16)


def spiked(entries, key, source, target, parts, factor):
    def block_of(axis_at):
        return (jnp.arange(entries.shape[axis_at]) // (entries.shape[axis_at] // parts)).reshape((-1,) + (1,) * (entries.ndim - 1 - axis_at))

    first = jax.random.permutation(key, parts)[block_of(target)]
    other_side = (block_of(target) + parts // 2) % parts
    return jnp.where((block_of(source) == first) | (block_of(source) == other_side), factor * entries, entries)


def shard_levels(own_key, dims, pieces, low, high):
    def one(axis_at, blocks):
        draws = jax.random.uniform(jax.random.fold_in(jax.random.fold_in(own_key, 6), axis_at), (blocks,), jnp.float32, low / len(pieces), high / len(pieces))
        return jnp.repeat(jnp.exp(draws), dims[axis_at] // blocks).reshape((-1,) + (1,) * (len(dims) - axis_at - 1))

    loudness = one(*pieces[0])
    for cut in pieces[1:]:
        loudness = loudness * one(*cut)
    return loudness


def bell_draw(own_key, dims, spread, reach, pieces=(), dtype=jnp.bfloat16):
    entries = jax.random.normal(own_key, dims, jnp.float32) * spread
    if len(pieces) > 0:
        entries = shard_levels(own_key, dims, pieces, -0.22, 0.18) * entries
    return jnp.clip(entries, min=-reach, max=reach).astype(dtype)


def gaussian_with(key, dims, scale, bound, shards, heavy, kind=jnp.bfloat16):
    result = scale * jax.random.normal(key, dims, jnp.float32)
    if shards:
        result = result * shard_levels(key, dims, shards, -0.22, 0.18)
    return jnp.clip(spiked(result, jax.random.fold_in(key, 3), *heavy), -bound, bound).astype(kind)


def setup_inputs(seed: int = 0) -> dict:
    key_list = jax.random.split(jax.random.key(seed), 11)
    inputs = gaussian_with(key_list[0], (BATCH_SEQUENCES, SEQUENCE_LENGTH, MODEL_WIDTH), 1.0, 6.0, ((0, 16), (1, 16)), (0, 2, 16, 2.0))
    query_saved = draw_query_saved(jax.random.fold_in(key_list[10], 71), 0)
    key_saved = draw_key_saved(jax.random.fold_in(key_list[10], 71), 0)
    value_saved = bell_draw(key_list[3], (BATCH_SEQUENCES, SEQUENCE_LENGTH, DKV), 1.0, 6.0, ((0, 16), (1, 16)))
    grad_out = bell_draw(key_list[4], (BATCH_SEQUENCES, SEQUENCE_LENGTH, DQ), 1.0, 6.0, ((0, 16), (1, 16)))
    value_weight = bell_draw(key_list[5], (MODEL_WIDTH, DKV), (16.0 / DKV ** 0.5), 6.0, ((0, 16),))
    query_down_weight = bell_draw(key_list[6], (R, MODEL_WIDTH), R ** -0.5, 1.5)
    up_q = bell_draw(key_list[7], (R, DQ), 0.3, 4.0)
    value_down_weight = bell_draw(key_list[8], (R, MODEL_WIDTH), R ** -0.5, 1.5)
    up_v = bell_draw(key_list[9], (R, DKV), DKV ** -0.5, 0.25)
    return {"inputs": inputs, "query_saved": query_saved, "key_saved": key_saved, "value_saved": value_saved, "grad_out": grad_out, "value_weight": value_weight, "query_down_weight": query_down_weight, "up_q": up_q, "value_down_weight": value_down_weight, "up_v": up_v}


adapter_scale = 2.0

def attend_back(query_rows, gout_rows, key_rows, value_rows):
    highest = lax.Precision.HIGHEST
    score_scale = 1.0 / math.sqrt(query_rows.shape[-1])
    length = query_rows.shape[0]
    scores = jnp.einsum('tkgd,skd->kgts', query_rows, key_rows, precision=highest) * score_scale
    allowed = jnp.arange(length)[None, :] <= jnp.arange(length)[:, None]
    scores = jnp.where(allowed, scores, -jnp.inf)
    row_max = lax.optimization_barrier(jnp.max(scores, axis=-1, keepdims=True))
    weights = jnp.exp(scores - row_max)
    probs = weights / lax.optimization_barrier(jnp.sum(weights, axis=-1, keepdims=True))
    probs_b = lax.optimization_barrier(probs.astype(jnp.bfloat16)).astype(jnp.float32)
    attn_out = jnp.einsum('kgts,skd->tkgd', probs_b, value_rows, precision=highest)
    delta = lax.optimization_barrier(jnp.sum(gout_rows * attn_out, axis=-1))
    dprob = jnp.einsum('tkgd,skd->kgts', gout_rows, value_rows, precision=highest)
    dscore = probs * (dprob - jnp.transpose(delta, (1, 2, 0))[..., None])
    dscore = lax.optimization_barrier(dscore.astype(jnp.bfloat16)).astype(jnp.float32)
    dquery = jnp.einsum('kgts,skd->tkgd', dscore, key_rows, precision=highest) * score_scale
    dvalue = jnp.einsum('kgts,tkgd->skd', probs_b, gout_rows, precision=highest)
    return (dquery.reshape(length, -1), dvalue.reshape(length, -1))

def reference(inputs, query_saved, key_saved, value_saved, grad_out, value_weight, query_down_weight, up_q, value_down_weight, up_v):
    half_q = DQ // 2
    half_kv = DKV // 2
    half_head_count = LOCAL_KV_HEADS // 2
    head_group_ratio = LOCAL_Q_HEADS // LOCAL_KV_HEADS
    group_count = BATCH_SEQUENCES * SEQUENCE_LENGTH // GROUP
    dquery_parts = []
    dvalue_parts = []
    for half_index in range(2):
        roll_by = 2 * TOK_DEV * half_index

        def take_half(array, width):
            part_cols = array[:, :, half_index * width:(half_index + 1) * width].astype(jnp.float32)
            return jnp.roll(part_cols, -roll_by, axis=1).reshape(group_count, GROUP, width)
        query_groups = take_half(query_saved, half_q)
        gout_groups = take_half(grad_out, half_q)
        key_groups = take_half(key_saved, half_kv)
        value_groups = take_half(value_saved, half_kv)

        def one_group(operands):
            query_group, gout_group, key_group, value_group = operands
            return attend_back(query_group.reshape(GROUP, half_head_count, head_group_ratio, HEAD_WIDTH), gout_group.reshape(GROUP, half_head_count, head_group_ratio, HEAD_WIDTH), key_group.reshape(GROUP, half_head_count, HEAD_WIDTH), value_group.reshape(GROUP, half_head_count, HEAD_WIDTH))
        dquery_groups, dvalue_groups = lax.map(one_group, (query_groups, gout_groups, key_groups, value_groups))
        dquery_parts.append(jnp.roll(dquery_groups.reshape(BATCH_SEQUENCES, SEQUENCE_LENGTH, half_q), roll_by, axis=1))
        dvalue_parts.append(jnp.roll(dvalue_groups.reshape(BATCH_SEQUENCES, SEQUENCE_LENGTH, half_kv), roll_by, axis=1))
    grad_query = jnp.concatenate(dquery_parts, axis=-1).astype(jnp.bfloat16).reshape(BATCH_SEQUENCES * SEQUENCE_LENGTH, DQ)
    grad_value = jnp.concatenate(dvalue_parts, axis=-1).astype(jnp.bfloat16).reshape(BATCH_SEQUENCES * SEQUENCE_LENGTH, DKV)
    flat_inputs = inputs.reshape(BATCH_SEQUENCES * SEQUENCE_LENGTH, MODEL_WIDTH)
    query_adapter_code = jnp.dot(grad_query, up_q.T, preferred_element_type=jnp.float32).astype(jnp.bfloat16)
    value_adapter_code = jnp.dot(grad_value, up_v.T, preferred_element_type=jnp.float32).astype(jnp.bfloat16)
    hidden_q = jnp.dot(flat_inputs, query_down_weight.T, preferred_element_type=jnp.float32).astype(jnp.bfloat16)
    hidden_v = jnp.dot(flat_inputs, value_down_weight.T, preferred_element_type=jnp.float32).astype(jnp.bfloat16)
    gradient_scale = adapter_scale / math.sqrt(BATCH_SEQUENCES * SEQUENCE_LENGTH)
    grad_down_q = gradient_scale * jnp.dot(query_adapter_code.T, flat_inputs, preferred_element_type=jnp.float32)
    grad_up_q = gradient_scale * jnp.dot(hidden_q.T, grad_query, preferred_element_type=jnp.float32)
    grad_down_v = gradient_scale * jnp.dot(value_adapter_code.T, flat_inputs, preferred_element_type=jnp.float32)
    grad_up_v = gradient_scale * jnp.dot(hidden_v.T, grad_value, preferred_element_type=jnp.float32)
    value_gradient_path = jnp.dot(grad_value, value_weight.T, preferred_element_type=jnp.float32)
    adapter_gradient_path = jnp.dot(query_adapter_code, query_down_weight, preferred_element_type=jnp.float32) + jnp.dot(value_adapter_code, value_down_weight, preferred_element_type=jnp.float32)
    input_gradient = (value_gradient_path + adapter_scale * adapter_gradient_path).astype(jnp.bfloat16).reshape(BATCH_SEQUENCES, SEQUENCE_LENGTH, MODEL_WIDTH)
    return (grad_down_q, grad_up_q, grad_down_v, grad_up_v, input_gradient)
```

```python
import functools
import math

import jax
import jax.numpy as jnp
from jax import lax
from jax.experimental import pallas as pl
from jax.experimental.pallas import tpu as pltpu
from jax.sharding import PartitionSpec as P

MESH = pl.DeviceIdType.MESH
F32 = jnp.float32
BF16 = jnp.bfloat16

CTX = 16
DP = 16
T = 192
D = 128
LANES = 4 * T
QUADS = 8
WIDTH = 8192
SHARD = WIDTH // DP
DQ = 4096
DKV = 512
ADAPTER_SCALE = 2.0
CHUNK = 32


def nt(a, b):
    return lax.dot_general(a, b, (((1,), (1,)), ((), ())), preferred_element_type=F32)


def nn(a, b):
    return jnp.dot(a, b, preferred_element_type=F32)


def kernel(
    x_hbm,
    q_hbm,
    k_hbm,
    v_hbm,
    g_hbm,
    w_hbm,
    qdw_hbm,
    upq_hbm,
    vdw_hbm,
    upv_hbm,
    down_q_out,
    up_q_out,
    down_v_out,
    up_v_out,
    dx_hbm,
    x,
    q,
    g,
    kvw,
    w,
    dw,
    upq,
    upv,
    bias,
    s_buf,
    dp_buf,
    pb_buf,
    ds_buf,
    kt,
    dv_acc,
    dv_own,
    dv_snd,
    dv_rcv,
    gq,
    gv,
    hid,
    ht4,
    codes,
    term_q,
    term_v,
    rcv_q,
    rcv_v,
    rs_src,
    rs_rcv,
    ag,
    dx,
    loc_sem,
    kv_ssem,
    kv_rsem,
    w_ssem,
    w_rsem,
    dv_ssem,
    dv_rsem,
    t_ssem,
    t_rsem,
    r_ssem,
    r_rsem,
    out_sem,
):
    c = lax.axis_index("ctx")
    p = lax.axis_index("dp")
    right = lax.rem(c + 1, CTX)
    scale = 1.0 / math.sqrt(D)
    exp2_scale = scale * math.log2(math.e)

    def remote(src, dst, ssem, rsem, ctx, dp):
        return pltpu.make_async_remote_copy(
            src_ref=src,
            dst_ref=dst,
            send_sem=ssem,
            recv_sem=rsem,
            device_id=(ctx, dp),
            device_id_type=MESH,
        )

    loads = []

    def load(src, dst):
        copy = pltpu.make_async_copy(src, dst, loc_sem.at[len(loads)])
        copy.start()
        loads.append(copy)
        return copy

    kv_loads = []
    for half in range(2):
        for which, ref in ((0, k_hbm), (1, v_hbm)):
            for head in range(2):
                col = (half * 2 + head) * D
                kv_loads.append(load(ref.at[:, col : col + D], kvw.at[half, 0, which, head]))
    dw_loads = [load(qdw_hbm, dw.at[0:16]), load(vdw_hbm, dw.at[16:32])]
    x_load = load(x_hbm, x)
    q_load = load(q_hbm, q)
    g_load = load(g_hbm, g)
    up_loads = [load(upq_hbm, upq), load(upv_hbm, upv)]
    w_load = load(w_hbm, w.at[p])

    with jax.named_scope("greet"):
        barrier = pltpu.get_barrier_semaphore()

        def greet(off, carry):
            pl.semaphore_signal(
                barrier, inc=1, device_id=(lax.rem(c + off, CTX), p), device_id_type=MESH
            )
            pl.semaphore_signal(
                barrier, inc=1, device_id=(c, lax.rem(p + off, DP)), device_id_type=MESH
            )
            return carry

        lax.fori_loop(1, 16, greet, 0)
        pl.semaphore_wait(barrier, 30)

    lags = (lax.rem(c, 4), lax.rem(c + 2, 4))
    parity = lax.rem(c, 2)
    first_half = lax.rem(c, 4) // 2
    second_half = 1 - first_half

    def kv_copy(half, slot):
        return remote(
            kvw.at[half, slot],
            kvw.at[half, slot + 1],
            kv_ssem.at[half, slot],
            kv_rsem.at[half, slot + 1],
            right,
            p,
        )

    def kv_arrived(half, slot):
        remote(
            kvw.at[half, slot],
            kvw.at[half, slot],
            kv_ssem.at[half, slot],
            kv_rsem.at[half, slot],
            right,
            p,
        ).wait_recv()

    with jax.named_scope("kv_send"):
        for copy in kv_loads:
            copy.wait()
        for half in range(2):

            @pl.when(lags[half] < 3)
            def _(half=half):
                kv_copy(half, 0).start()

    core = lax.rem(p, 2)
    px = lax.rem(p // 2, 4)
    py = p // 8

    def at(dy, dx_, dc):
        yy = lax.rem(py + dy, 2)
        xx = lax.rem(px + dx_ + 4, 4)
        cc = lax.rem(core + dc, 2)
        return yy * 8 + xx * 2 + cc

    x_up, x_dn, y_nb, sib = at(0, 1, 0), at(0, -1, 0), at(1, 0, 0), at(0, 0, 1)
    origin = [at(0, -1, 0), at(0, 1, 0), at(1, 0, 0), at(0, 2, 0), at(1, -1, 0), at(1, 1, 0), at(1, 2, 0)]
    origin = origin + [at(0, 0, 1)] + [
        at(0, -1, 1),
        at(0, 1, 1),
        at(1, 0, 1),
        at(0, 2, 1),
        at(1, -1, 1),
        at(1, 1, 1),
        at(1, 2, 1),
    ]

    def w_copy(kind, shard, target, src=None):
        block = w.at[shard]
        return remote(
            block if src is None else src, block, w_ssem.at[kind], w_rsem.at[kind], c, target
        )

    def w_arrived(kind):
        remote(
            w.at[origin[kind]], w.at[origin[kind]], w_ssem.at[kind], w_rsem.at[kind], c, sib
        ).wait_recv()

    w_sends = {
        0: w_copy(0, p, x_up, w_hbm),
        1: w_copy(1, p, x_dn, w_hbm),
        2: w_copy(2, p, y_nb, w_hbm),
        7: w_copy(7, p, sib, w_hbm),
        3: w_copy(3, origin[1], x_dn),
        4: w_copy(4, origin[2], x_up),
        5: w_copy(5, origin[1], y_nb),
        6: w_copy(6, origin[3], y_nb),
    }
    for i in range(7):
        w_sends[8 + i] = w_copy(8 + i, origin[i], sib)
    for kind in (0, 1, 2, 7):
        w_sends[kind].start()

    with jax.named_scope("bias"):
        row = lax.broadcasted_iota(jnp.int32, (T, LANES), 0)
        lane = lax.broadcasted_iota(jnp.int32, (T, LANES), 1)
        turn = (
            (lane >= T).astype(jnp.int32)
            + (lane >= 2 * T).astype(jnp.int32)
            + (lane >= 3 * T).astype(jnp.int32)
        )
        bias[...] = jnp.where(row <= lane - turn * T, 0.0, -jnp.inf).astype(F32)

    with jax.named_scope("hidden"):
        for copy in dw_loads:
            copy.wait()
        x_load.wait()

        def hidden_step(i, acc):
            cols = pl.ds(pl.multiple_of(i * 1024, 1024), 1024)
            return acc + nt(dw[:, cols], x[:, cols])

        hidden = lax.fori_loop(0, 8, hidden_step, jnp.zeros((32, T), F32))
        hid[...] = jnp.zeros_like(hid)
        hid[:, 0:T] = hidden.astype(BF16).astype(F32)
        ht4[...] = jnp.zeros_like(ht4)
        padded = hid[0:16, :]
        turned = pltpu.roll(padded, 64, 1)
        ht4[0:16, 0:256] = padded.astype(BF16)
        ht4[16:32, 128:384] = turned.astype(BF16)
        ht4[32:48, 384:640] = padded.astype(BF16)
        ht4[48:64, 512:768] = turned.astype(BF16)

    with jax.named_scope("kv_forward_1"):
        for half in range(2):

            @pl.when(lags[half] >= 1)
            def _(half=half):
                kv_arrived(half, 1)

            @pl.when((lags[half] >= 1) & (lags[half] <= 2))
            def _(half=half):
                kv_copy(half, 1).start()

        q_load.wait()
        g_load.wait()

    def four_heads(ref, quad):
        block = ref[:, pl.ds(pl.multiple_of(quad * 512, 512), 512)]
        return jnp.concatenate([block[:, i * D : (i + 1) * D] for i in range(4)], axis=0)

    def attend(half, kv, nk):
        n = nk * T

        keys = kvw[half, 0:nk, 0, kv].reshape(n, D)
        kt[:, 0:n] = keys.T
        dv_acc[0:n] = jnp.zeros((n, D), F32)

        def quad_step(i, carry):
            quad = half * 4 + kv * 2 + i
            q4 = four_heads(q, quad)
            top = None
            for d in range(nk):
                s = nt(kvw[half, d, 0, kv], q4)
                if d == 0:
                    s = s + bias[...]
                s_buf[d * T : (d + 1) * T] = s
                m = jnp.max(s, axis=0, keepdims=True)
                top = m if top is None else jnp.maximum(top, m)
            g4 = four_heads(g, quad)
            for d in range(nk):
                dp_buf[d * T : (d + 1) * T] = nt(kvw[half, d, 1, kv], g4)

            def exp_step(j, sums):
                rows = pl.ds(pl.multiple_of(j * CHUNK, CHUNK), CHUNK)
                e = jnp.exp2((s_buf[rows] - top) * exp2_scale)
                s_buf[rows] = e
                return (
                    sums[0] + jnp.sum(e.reshape(CHUNK // 8, 8, LANES), axis=0),
                    sums[1] + jnp.sum((e * dp_buf[rows]).reshape(CHUNK // 8, 8, LANES), axis=0),
                )

            zero = jnp.zeros((8, LANES), F32)
            total, weighted = lax.fori_loop(0, n // CHUNK, exp_step, (zero, zero), unroll=True)
            inv = 1.0 / jnp.sum(total, axis=0, keepdims=True)
            delta = jnp.sum(weighted, axis=0, keepdims=True) * inv

            def grad_step(j, carry):
                rows = pl.ds(pl.multiple_of(j * CHUNK, CHUNK), CHUNK)
                probs = s_buf[rows] * inv
                pb_buf[rows] = probs.astype(BF16)
                ds_buf[rows] = (probs * (dp_buf[rows] - delta)).astype(BF16)
                return carry

            lax.fori_loop(0, n // CHUNK, grad_step, 0, unroll=True)
            dv_acc[0:n] += nn(pb_buf[0:n], g4)
            gq[quad] = (nn(kt[:, 0:n], ds_buf[0:n]) * scale).astype(BF16)
            return carry

        lax.fori_loop(0, 2, quad_step, 0)
        dv_own[half, kv] = dv_acc[0:T]
        for d in range(1, nk):
            dv_snd[half, d - 1, kv] = dv_acc[d * T : (d + 1) * T].astype(BF16)
            dv_copy(half, d, kv).start()

    def dv_copy(half, d, kv):
        return remote(
            dv_snd.at[half, d - 1, kv],
            dv_rcv.at[half, d - 1, kv],
            dv_ssem.at[half, d - 1, kv],
            dv_rsem.at[half, d - 1, kv],
            lax.rem(c + CTX - d, CTX),
            p,
        )

    def first_step(kv, carry):
        @pl.when(parity == 0)
        def _():
            attend(first_half, kv, 1)

        @pl.when(parity == 1)
        def _():
            attend(first_half, kv, 2)

        return carry

    with jax.named_scope("attend_first"):
        lax.fori_loop(0, 2, first_step, 0)

    with jax.named_scope("kv_forward_2"):
        kv_arrived(second_half, 2)

        @pl.when(parity == 0)
        def _():
            kv_copy(second_half, 2).start()

    with jax.named_scope("w_forward_1"):
        for kind in (0, 1, 2):
            w_arrived(kind)
        for kind in (3, 4, 5, 8, 9, 10):
            w_sends[kind].start()

    with jax.named_scope("kv_last"):
        @pl.when(parity == 1)
        def _():
            kv_arrived(second_half, 3)

    def second_step(kv, carry):
        @pl.when(parity == 0)
        def _():
            attend(second_half, kv, 3)

        @pl.when(parity == 1)
        def _():
            attend(second_half, kv, 4)

        @pl.when(kv == 0)
        def _():
            with jax.named_scope("w_forward_2"):
                for kind in (3, 4, 5):
                    w_arrived(kind)
                for kind in (6, 11, 12, 13):
                    w_sends[kind].start()

        return carry

    with jax.named_scope("attend_second"):
        lax.fori_loop(0, 2, second_step, 0)

    with jax.named_scope("query_terms"):
        for copy in up_loads:
            copy.wait()
        flat_gq = gq[...].reshape(QUADS * D, LANES)
        up4 = jnp.concatenate(
            [
                jnp.concatenate(
                    [upq[:, (4 * i + j) * D : (4 * i + j + 1) * D] for i in range(QUADS)], axis=1
                )
                for j in range(4)
            ],
            axis=0,
        )
        r = nn(up4, flat_gq)
        code_q = (
            r[0:16, 0:256]
            + pltpu.roll(r[16:32, 128:384], 192, 1)
            + r[32:48, 384:640]
            + pltpu.roll(r[48:64, 512:768], 192, 1)
        )
        codes[...] = jnp.zeros_like(codes)
        codes[0:16, :] = code_q
        code_qt = codes[0:16, 0:T].astype(BF16)
        up_terms = nt(ht4[...], flat_gq)
        for i in range(DP):
            lo = 32 * (i % 2)
            col = D * (i // 2)
            term_q[i, :, 512:640] = up_terms[lo : lo + 16, col : col + D].astype(BF16)
            term_q[i, :, 640:768] = up_terms[lo + 16 : lo + 32, col : col + D].astype(BF16)

    def down_terms(term, code):
        def step(i, carry):
            cols = pl.ds(pl.multiple_of(i * SHARD, SHARD), SHARD)
            term[i, :, 0:SHARD] = nn(code, x[:, cols]).astype(BF16)
            return carry

        lax.fori_loop(0, DP, step, 0)

    def term_copy(which, off):
        target = lax.rem(p + off, DP)
        term, rcv = ((term_q, rcv_q), (term_v, rcv_v))[which]
        return remote(
            term.at[target],
            rcv.at[off],
            t_ssem.at[which, off],
            t_rsem.at[which, off],
            c,
            target,
        )

    def each(fn):
        def step(off, carry):
            fn(off)
            return carry

        lax.fori_loop(1, 16, step, 0)

    with jax.named_scope("query_down"):
        down_terms(term_q, code_qt)
        each(lambda off: term_copy(0, off).start())
        rcv_q[0] = term_q[p]

    with jax.named_scope("w_forward_3"):
        w_arrived(6)
        w_sends[14].start()

    with jax.named_scope("value_gradient"):
        for half in range(2):
            for d in range(1, 4):

                @pl.when(lags[half] + d <= 3)
                def _(half=half, d=d):
                    for kv in range(2):
                        dv_copy(half, d, kv).wait_recv()
                        dv_own[half, kv] += dv_rcv[half, d - 1, kv].astype(F32)

            for kv in range(2):
                col = (half * 2 + kv) * D
                gv[:, col : col + D] = dv_own[half, kv].astype(BF16)

        code_vt = nt(upv[...], gv[...])
        codes[16:32, 0:T] = code_vt
        code_vt = code_vt.astype(BF16)
        hidden_v = hid[16:32, 0:T].astype(BF16)
        up_v_terms = nn(hidden_v, gv[...])
        for i in range(DP):
            col = D * (i // 4)
            term_v[i, :, 512:640] = up_v_terms[:, col : col + D].astype(BF16)
        down_terms(term_v, code_vt)
        each(lambda off: term_copy(1, off).start())
        rcv_v[0] = term_v[p]

    with jax.named_scope("w_wait"):
        w_load.wait()
        for kind in range(7, 15):
            w_arrived(kind)
        code = (ADAPTER_SCALE * codes[...].astype(BF16).astype(F32)).T
        code = code[0:T, :].astype(BF16)

    def out_copy(i):
        cols = pl.ds(pl.multiple_of(i * SHARD, SHARD), SHARD)
        return pltpu.make_async_copy(dx.at[:, cols], dx_hbm.at[:, cols], out_sem.at[i])

    def dx_step(i, carry):
        cols = pl.ds(pl.multiple_of(i * SHARD, SHARD), SHARD)
        dx[:, cols] = (nt(gv[...], w[i]) + nn(code, dw[:, cols])).astype(BF16)
        out_copy(i).start()
        return carry

    with jax.named_scope("dx_1"):
        lax.fori_loop(0, 8, dx_step, 0)

    with jax.named_scope("sum_dp"):
        each(lambda off: term_copy(0, off).wait_recv())
        each(lambda off: term_copy(1, off).wait_recv())
        rs_src[...] = jnp.zeros_like(rs_src)
        sum_q = jnp.sum(rcv_q[...].astype(F32), axis=0)
        sum_v = jnp.sum(rcv_v[...].astype(F32), axis=0)
        for j in range(6):
            rs_src[:, j, :] = sum_q[:, j * D : (j + 1) * D]
        for j in range(5):
            rs_src[:, 6 + j, :] = sum_v[:, j * D : (j + 1) * D]

    def row_copy(off):
        target = lax.rem(c + off, CTX)
        return remote(
            rs_src.at[target], rs_rcv.at[off], r_ssem.at[0, off], r_rsem.at[0, off], target, p
        )

    def sum_copy(off, src=None):
        target = lax.rem(c + off, CTX)
        return remote(ag.at[c], ag.at[c], r_ssem.at[1, off], r_rsem.at[1, off], target, p)

    def sum_arrived(off):
        src = lax.rem(c + CTX - off, CTX)
        remote(ag.at[src], ag.at[src], r_ssem.at[1, off], r_rsem.at[1, off], src, p).wait_recv()

    each(lambda off: row_copy(off).start())
    rs_rcv[0] = rs_src[c]

    with jax.named_scope("dx_2"):
        lax.fori_loop(8, 12, dx_step, 0)

    with jax.named_scope("sum_ctx"):
        each(lambda off: row_copy(off).wait_recv())
        gradient_scale = ADAPTER_SCALE / math.sqrt(DP * CTX * T)
        ag[c] = jnp.sum(rs_rcv[...], axis=0) * gradient_scale
        each(lambda off: sum_copy(off).start())

    with jax.named_scope("dx_3"):
        lax.fori_loop(12, 16, dx_step, 0)

    with jax.named_scope("outputs"):
        each(sum_arrived)
        for j in range(4):
            down_q_out[:, j * D : (j + 1) * D] = ag[:, j, :]
            down_v_out[:, j * D : (j + 1) * D] = ag[:, 6 + j, :]
        for j in range(2):
            up_q_out[:, j * D : (j + 1) * D] = ag[:, 4 + j, :]
        piece = ag[:, 10, :]
        for j in range(4):

            @pl.when(lax.rem(p, 4) == j)
            def _(j=j):
                up_v_out[...] = piece[:, 32 * j : 32 * (j + 1)]

    with jax.named_scope("drain"):
        def out_wait(i, carry):
            out_copy(i).wait()
            return carry

        lax.fori_loop(0, DP, out_wait, 0)
        for half in range(2):

            @pl.when(lags[half] < 3)
            def _(half=half):
                kv_copy(half, 0).wait_send()

            @pl.when((lags[half] >= 1) & (lags[half] <= 2))
            def _(half=half):
                kv_copy(half, 1).wait_send()

            for d in range(1, 4):

                @pl.when(lags[half] >= d)
                def _(half=half, d=d):
                    for kv in range(2):
                        dv_copy(half, d, kv).wait_send()

        @pl.when(parity == 0)
        def _():
            kv_copy(second_half, 2).wait_send()

        for kind in range(15):
            w_sends[kind].wait_send()

        def sent(off):
            term_copy(0, off).wait_send()
            term_copy(1, off).wait_send()
            row_copy(off).wait_send()
            sum_copy(off).wait_send()

        each(sent)


def on_device(
    inputs,
    query_saved,
    key_saved,
    value_saved,
    grad_out,
    value_weight,
    query_down_weight,
    up_q,
    value_down_weight,
    up_v,
):
    out = pl.pallas_call(
        kernel,
        out_shape=(
            jax.ShapeDtypeStruct((16, SHARD), F32),
            jax.ShapeDtypeStruct((16, DQ // DP), F32),
            jax.ShapeDtypeStruct((16, SHARD), F32),
            jax.ShapeDtypeStruct((16, DKV // DP), F32),
            jax.ShapeDtypeStruct((T, WIDTH), BF16),
        ),
        in_specs=[pl.BlockSpec(memory_space=pl.ANY)] * 10,
        out_specs=[pl.BlockSpec(memory_space=pltpu.VMEM)] * 4
        + [pl.BlockSpec(memory_space=pl.ANY)],
        scratch_shapes=[
            pltpu.VMEM((T, WIDTH), BF16),
            pltpu.VMEM((T, DQ), BF16),
            pltpu.VMEM((T, DQ), BF16),
            pltpu.VMEM((2, 4, 2, 2, T, D), BF16),
            pltpu.VMEM((DP, SHARD, DKV), BF16),
            pltpu.VMEM((32, WIDTH), BF16),
            pltpu.VMEM((16, DQ), BF16),
            pltpu.VMEM((16, DKV), BF16),
            pltpu.VMEM((T, LANES), F32),
            pltpu.VMEM((4 * T, LANES), F32),
            pltpu.VMEM((4 * T, LANES), F32),
            pltpu.VMEM((4 * T, LANES), BF16),
            pltpu.VMEM((4 * T, LANES), BF16),
            pltpu.VMEM((D, 4 * T), BF16),
            pltpu.VMEM((4 * T, D), F32),
            pltpu.VMEM((2, 2, T, D), F32),
            pltpu.VMEM((2, 3, 2, T, D), BF16),
            pltpu.VMEM((2, 3, 2, T, D), BF16),
            pltpu.VMEM((QUADS, D, LANES), BF16),
            pltpu.VMEM((T, DKV), BF16),
            pltpu.VMEM((32, 256), F32),
            pltpu.VMEM((64, LANES), BF16),
            pltpu.VMEM((32, 256), F32),
            pltpu.VMEM((DP, 16, 768), BF16),
            pltpu.VMEM((DP, 16, 640), BF16),
            pltpu.VMEM((DP, 16, 768), BF16),
            pltpu.VMEM((DP, 16, 640), BF16),
            pltpu.VMEM((CTX, 16, D), F32),
            pltpu.VMEM((CTX, 16, D), F32),
            pltpu.VMEM((CTX, 16, D), F32),
            pltpu.VMEM((T, WIDTH), BF16),
            pltpu.SemaphoreType.DMA((16,)),
            pltpu.SemaphoreType.DMA((2, 4)),
            pltpu.SemaphoreType.DMA((2, 4)),
            pltpu.SemaphoreType.DMA((15,)),
            pltpu.SemaphoreType.DMA((15,)),
            pltpu.SemaphoreType.DMA((2, 3, 2)),
            pltpu.SemaphoreType.DMA((2, 3, 2)),
            pltpu.SemaphoreType.DMA((2, 16)),
            pltpu.SemaphoreType.DMA((2, 16)),
            pltpu.SemaphoreType.DMA((2, 16)),
            pltpu.SemaphoreType.DMA((2, 16)),
            pltpu.SemaphoreType.DMA((16,)),
        ],
        compiler_params=pltpu.CompilerParams(
            collective_id=0, has_side_effects=True, vmem_limit_bytes=56 * 1024 * 1024
        ),
    )(
        inputs[0],
        query_saved[0],
        key_saved[0],
        value_saved[0],
        grad_out[0],
        value_weight,
        query_down_weight,
        up_q,
        value_down_weight,
        up_v,
    )
    return out[0], out[1], out[2], out[3], out[4][None]


def solution(mesh):
    in_specs = (
        P("dp", "ctx", None),
        P("dp", "ctx", None),
        P("dp", "ctx", None),
        P("dp", "ctx", None),
        P("dp", "ctx", None),
        P("dp", None),
        P(),
        P(),
        P(),
        P(),
    )
    out_specs = (P(None, "dp"), P(None, "dp"), P(None, "dp"), P(None, "dp"), P("dp", "ctx", None))
    return jax.shard_map(
        on_device, mesh=mesh, in_specs=in_specs, out_specs=out_specs, check_vma=False
    )
```

```python
import functools
import math

import jax
import jax.numpy as jnp
from jax import lax
from jax.experimental import pallas as pl
from jax.experimental.pallas import tpu as pltpu
from jax.sharding import PartitionSpec as P

MESH = pl.DeviceIdType.MESH
F32 = jnp.float32
BF16 = jnp.bfloat16

CTX = 16
DP = 16
T = 192
D = 128
LANES = 4 * T
QUADS = 8
WIDTH = 8192
SHARD = WIDTH // DP
DQ = 4096
DKV = 512
ADAPTER_SCALE = 2.0
CHUNK = 32


def nt(a, b):
    return lax.dot_general(a, b, (((1,), (1,)), ((), ())), preferred_element_type=F32)


def nn(a, b):
    return jnp.dot(a, b, preferred_element_type=F32)


def kernel(
    x_hbm,
    q_hbm,
    k_hbm,
    v_hbm,
    g_hbm,
    w_hbm,
    qdw_hbm,
    upq_hbm,
    vdw_hbm,
    upv_hbm,
    ag_out,
    dx,
    x,
    q,
    g,
    kvw,
    w,
    dw,
    upq,
    upv,
    bias,
    s_buf,
    dp_buf,
    pb_buf,
    ds_buf,
    kt,
    dv_acc,
    dv_own,
    dv_snd,
    dv_rcv,
    gq,
    gv,
    hid,
    ht4,
    codes,
    term_q,
    term_v,
    rcv_q,
    rcv_v,
    rs_src,
    rs_rcv,
    ag,
    loc_sem,
    kv_ssem,
    kv_rsem,
    w_ssem,
    w_rsem,
    dv_ssem,
    dv_rsem,
    t_ssem,
    t_rsem,
    r_ssem,
    r_rsem,
):
    c = lax.axis_index("ctx")
    p = lax.axis_index("dp")
    right = lax.rem(c + 1, CTX)
    scale = 1.0 / math.sqrt(D)
    exp2_scale = scale * math.log2(math.e)

    def remote(src, dst, ssem, rsem, ctx, dp):
        return pltpu.make_async_remote_copy(
            src_ref=src,
            dst_ref=dst,
            send_sem=ssem,
            recv_sem=rsem,
            device_id=(ctx, dp),
            device_id_type=MESH,
        )

    loads = []

    def load(src, dst):
        copy = pltpu.make_async_copy(src, dst, loc_sem.at[len(loads)])
        copy.start()
        loads.append(copy)
        return copy

    kv_loads = []
    for half in range(2):
        for which, ref in ((0, k_hbm), (1, v_hbm)):
            for head in range(2):
                col = (half * 2 + head) * D
                kv_loads.append(load(ref.at[:, col : col + D], kvw.at[half, 0, head, which]))
    dw_loads = [load(qdw_hbm, dw.at[0:16]), load(vdw_hbm, dw.at[16:32])]
    x_load = load(x_hbm, x)
    q_load = load(q_hbm, q)
    g_load = load(g_hbm, g)
    up_loads = [load(upq_hbm, upq), load(upv_hbm, upv)]
    w_load = load(w_hbm, w.at[p])

    with jax.named_scope("greet"):
        barrier = pltpu.get_barrier_semaphore()

        def greet(off, carry):
            pl.semaphore_signal(
                barrier, inc=1, device_id=(lax.rem(c + off, CTX), p), device_id_type=MESH
            )
            pl.semaphore_signal(
                barrier, inc=1, device_id=(c, lax.rem(p + off, DP)), device_id_type=MESH
            )
            return carry

        lax.fori_loop(1, 16, greet, 0)
        pl.semaphore_signal(
            barrier,
            inc=1,
            device_id=(lax.rem(c + 8, CTX), lax.rem(p + 8, DP)),
            device_id_type=MESH,
        )
        pl.semaphore_wait(barrier, 31)

    lags = (lax.rem(c, 4), lax.rem(c + 2, 4))
    parity = lax.rem(c, 2)
    first_half = lax.rem(c, 4) // 2
    second_half = 1 - first_half

    def kv_copy(half, slot, kv):
        return remote(
            kvw.at[half, slot, kv],
            kvw.at[half, slot + 1, kv],
            kv_ssem.at[half, slot, kv],
            kv_rsem.at[half, slot + 1, kv],
            right,
            p,
        )

    def kv_arrived(half, slot, kv):
        remote(
            kvw.at[half, slot, kv],
            kvw.at[half, slot, kv],
            kv_ssem.at[half, slot, kv],
            kv_rsem.at[half, slot, kv],
            right,
            p,
        ).wait_recv()

    with jax.named_scope("kv_send"):
        for copy in kv_loads:
            copy.wait()
        for kv in range(2):
            kv_copy(first_half, 0, kv).start()

    core = lax.rem(p, 2)
    px = lax.rem(p // 2, 4)
    py = p // 8

    def at(dy, dx_, dc):
        yy = lax.rem(py + dy, 2)
        xx = lax.rem(px + dx_ + 4, 4)
        cc = lax.rem(core + dc, 2)
        return yy * 8 + xx * 2 + cc

    x_up, x_dn, y_nb, sib = at(0, 1, 0), at(0, -1, 0), at(1, 0, 0), at(0, 0, 1)
    far = lax.rem(c + 8, CTX)
    rows = SHARD // 2
    own, up, dn, opp = p, x_up, x_dn, at(0, 2, 0)
    y_own, y_up, y_dn, y_opp = at(1, 0, 0), at(1, 1, 0), at(1, -1, 0), at(1, 2, 0)
    w_plan = [
        (own, dn, 2, c, x_up),
        (own, up, 2, c, x_dn),
        (own, y_own, 0, c, y_nb),
        (own, y_own, 1, far, y_nb),
        (own, sib, 2, c, sib),
        (up, opp, 0, c, x_dn),
        (dn, opp, 1, c, x_up),
        (up, y_up, 0, c, y_nb),
        (dn, y_dn, 0, far, y_nb),
        (y_own, y_up, 1, c, x_dn),
        (y_own, y_dn, 1, c, x_up),
        (opp, y_opp, 0, c, y_nb),
        (opp, y_opp, 1, far, y_nb),
        (dn, at(0, -1, 1), 2, c, sib),
        (up, at(0, 1, 1), 2, c, sib),
        (y_own, at(1, 0, 1), 2, c, sib),
        (opp, at(0, 2, 1), 2, c, sib),
        (y_up, at(1, 1, 1), 2, c, sib),
        (y_dn, at(1, -1, 1), 2, c, sib),
        (y_opp, at(1, 2, 1), 2, c, sib),
    ]

    def w_part(shard, part):
        return w.at[shard] if part == 2 else w.at[shard, part * rows : (part + 1) * rows]

    def w_copy(number):
        shard, _, part, ctx, target = w_plan[number]
        block = w_part(shard, part)
        src = block
        if number < 5:
            src = w_hbm if part == 2 else w_hbm.at[part * rows : (part + 1) * rows]
        return remote(src, block, w_ssem.at[number], w_rsem.at[number], ctx, target)

    def w_arrived(*numbers):
        for number in numbers:
            _, shard, part, ctx, target = w_plan[number]
            block = w_part(shard, part)
            remote(
                block, block, w_ssem.at[number], w_rsem.at[number], ctx, target
            ).wait_recv()

    def w_start(*numbers):
        for number in numbers:
            w_copy(number).start()

    def w_round_1():
        with jax.named_scope("w_round_1"):
            w_arrived(0, 1, 2, 3)
            w_start(5, 6, 7, 8, 9, 10, 13, 14, 15)

    def w_round_2():
        with jax.named_scope("w_round_2"):
            w_arrived(5, 6)
            w_start(11, 12, 16)

    w_start(2, 3, 0, 1, 4)

    with jax.named_scope("bias"):
        row = lax.broadcasted_iota(jnp.int32, (T, LANES), 0)
        lane = lax.broadcasted_iota(jnp.int32, (T, LANES), 1)
        turn = (
            (lane >= T).astype(jnp.int32)
            + (lane >= 2 * T).astype(jnp.int32)
            + (lane >= 3 * T).astype(jnp.int32)
        )
        bias[...] = jnp.where(row <= lane - turn * T, 0.0, -jnp.inf).astype(F32)

    with jax.named_scope("hidden"):
        for copy in dw_loads:
            copy.wait()
        x_load.wait()

        def hidden_step(i, acc):
            cols = pl.ds(pl.multiple_of(i * 1024, 1024), 1024)
            return acc + nt(dw[:, cols], x[:, cols])

        hidden = lax.fori_loop(0, 8, hidden_step, jnp.zeros((32, T), F32))
        hid[...] = jnp.zeros_like(hid)
        hid[:, 0:T] = hidden.astype(BF16).astype(F32)
        ht4[...] = jnp.zeros_like(ht4)
        padded = hid[0:16, :]
        turned = pltpu.roll(padded, 64, 1)
        ht4[0:16, 0:256] = padded.astype(BF16)
        ht4[16:32, 128:384] = turned.astype(BF16)
        ht4[32:48, 384:640] = padded.astype(BF16)
        ht4[48:64, 512:768] = turned.astype(BF16)

    q_load.wait()
    g_load.wait()

    def four_heads(ref, quad):
        block = ref[:, pl.ds(pl.multiple_of(quad * 512, 512), 512)]
        return jnp.concatenate([block[:, i * D : (i + 1) * D] for i in range(4)], axis=0)

    def attend(half, kv, nk, between=None):
        n = nk * T

        keys = kvw[half, 0:nk, kv, 0].reshape(n, D)
        kt[:, 0:n] = keys.T
        dv_acc[0:n] = jnp.zeros((n, D), F32)

        def quad_step(i, carry):
            if between is not None:
                pl.when(i == 1)(between)
            quad = half * 4 + kv * 2 + i
            q4 = four_heads(q, quad)
            top = None
            for d in range(nk):
                s = nt(kvw[half, d, kv, 0], q4)
                if d == 0:
                    s = s + bias[...]
                s_buf[d * T : (d + 1) * T] = s
                m = jnp.max(s, axis=0, keepdims=True)
                top = m if top is None else jnp.maximum(top, m)
            g4 = four_heads(g, quad)
            for d in range(nk):
                dp_buf[d * T : (d + 1) * T] = nt(kvw[half, d, kv, 1], g4)

            def exp_step(j, sums):
                rows = pl.ds(pl.multiple_of(j * CHUNK, CHUNK), CHUNK)
                e = jnp.exp2((s_buf[rows] - top) * exp2_scale)
                s_buf[rows] = e
                return (
                    sums[0] + jnp.sum(e.reshape(CHUNK // 8, 8, LANES), axis=0),
                    sums[1] + jnp.sum((e * dp_buf[rows]).reshape(CHUNK // 8, 8, LANES), axis=0),
                )

            zero = jnp.zeros((8, LANES), F32)
            total, weighted = lax.fori_loop(0, n // CHUNK, exp_step, (zero, zero), unroll=True)
            inv = 1.0 / jnp.sum(total, axis=0, keepdims=True)
            delta = jnp.sum(weighted, axis=0, keepdims=True) * inv

            def grad_step(j, carry):
                rows = pl.ds(pl.multiple_of(j * CHUNK, CHUNK), CHUNK)
                probs = s_buf[rows] * inv
                pb_buf[rows] = probs.astype(BF16)
                ds_buf[rows] = (probs * (dp_buf[rows] - delta)).astype(BF16)
                return carry

            lax.fori_loop(0, n // CHUNK, grad_step, 0, unroll=True)
            dv_acc[0:n] += nn(pb_buf[0:n], g4)
            gq[quad] = (nn(kt[:, 0:n], ds_buf[0:n]) * scale).astype(BF16)
            return carry

        lax.fori_loop(0, 2, quad_step, 0)
        dv_own[half, kv] = dv_acc[0:T]
        for d in range(1, nk):
            dv_snd[half, d - 1, kv] = dv_acc[d * T : (d + 1) * T].astype(BF16)
            dv_copy(half, d, kv).start()

    def dv_copy(half, d, kv):
        return remote(
            dv_snd.at[half, d - 1, kv],
            dv_rcv.at[half, d - 1, kv],
            dv_ssem.at[half, d - 1, kv],
            dv_rsem.at[half, d - 1, kv],
            lax.rem(c + CTX - d, CTX),
            p,
        )

    @pl.when(parity == 0)
    def _():
        def first_step(kv, carry):
            attend(first_half, kv, 1)

            @pl.when(kv == 0)
            def _():
                kv_copy(second_half, 0, 0).start()

            return carry

        with jax.named_scope("even_first"):
            lax.fori_loop(0, 2, first_step, 0)
        with jax.named_scope("even_pass"):
            kv_arrived(second_half, 1, 0)
            kv_copy(second_half, 1, 0).start()
            kv_arrived(second_half, 2, 0)
            kv_copy(second_half, 2, 0).start()
            kv_copy(second_half, 0, 1).start()
            kv_arrived(second_half, 1, 1)
            kv_copy(second_half, 1, 1).start()

        def second_step(kv, carry):
            @pl.when(kv == 1)
            def _():
                kv_arrived(second_half, 2, 1)
                kv_copy(second_half, 2, 1).start()
                w_round_1()

            attend(second_half, kv, 3)
            return carry

        with jax.named_scope("even_second"):
            lax.fori_loop(0, 2, second_step, 0)
        w_round_2()

    @pl.when(parity == 1)
    def _():
        def first_step(kv, carry):
            kv_arrived(first_half, 1, kv)
            kv_copy(first_half, 1, kv).start()
            attend(first_half, kv, 2)
            return carry

        with jax.named_scope("odd_first"):
            lax.fori_loop(0, 2, first_step, 0)

        def second_step(kv, carry):
            for slot in (1, 2, 3):
                kv_arrived(second_half, slot, kv)

            def between():
                pl.when(kv == 0)(w_round_1)
                pl.when(kv == 1)(w_round_2)

            attend(second_half, kv, 4, between)
            return carry

        with jax.named_scope("odd_second"):
            lax.fori_loop(0, 2, second_step, 0)

    with jax.named_scope("query_terms"):
        for copy in up_loads:
            copy.wait()
        flat_gq = gq[...].reshape(QUADS * D, LANES)
        up4 = jnp.concatenate(
            [
                jnp.concatenate(
                    [upq[:, (4 * i + j) * D : (4 * i + j + 1) * D] for i in range(QUADS)], axis=1
                )
                for j in range(4)
            ],
            axis=0,
        )
        r = nn(up4, flat_gq)
        code_q = (
            r[0:16, 0:256]
            + pltpu.roll(r[16:32, 128:384], 192, 1)
            + r[32:48, 384:640]
            + pltpu.roll(r[48:64, 512:768], 192, 1)
        )
        codes[...] = jnp.zeros_like(codes)
        codes[0:16, :] = code_q
        code_qt = codes[0:16, 0:T].astype(BF16)
        up_terms = nt(ht4[...], flat_gq)
        for i in range(DP):
            lo = 32 * (i % 2)
            col = D * (i // 2)
            term_q[i, :, 512:640] = up_terms[lo : lo + 16, col : col + D].astype(BF16)
            term_q[i, :, 640:768] = up_terms[lo + 16 : lo + 32, col : col + D].astype(BF16)

    def down_terms(term, code):
        def step(i, carry):
            cols = pl.ds(pl.multiple_of(i * SHARD, SHARD), SHARD)
            term[i, :, 0:SHARD] = nn(code, x[:, cols]).astype(BF16)
            return carry

        lax.fori_loop(0, DP, step, 0, unroll=4)

    def term_copy(which, off):
        target = lax.rem(p + off, DP)
        term, rcv = ((term_q, rcv_q), (term_v, rcv_v))[which]
        return remote(
            term.at[target],
            rcv.at[off],
            t_ssem.at[which, off],
            t_rsem.at[which, off],
            c,
            target,
        )

    def each(fn):
        def step(off, carry):
            fn(off)
            return carry

        lax.fori_loop(1, 16, step, 0)

    with jax.named_scope("query_down"):
        down_terms(term_q, code_qt)
        each(lambda off: term_copy(0, off).start())
        rcv_q[0] = term_q[p]

    with jax.named_scope("w_round_3"):
        w_arrived(7, 8, 9, 10)
        w_start(17, 18)
        w_arrived(11, 12)
        w_start(19)

    with jax.named_scope("value_gradient"):
        for half in range(2):
            for d in range(1, 4):

                @pl.when(lags[half] + d <= 3)
                def _(half=half, d=d):
                    for kv in range(2):
                        dv_copy(half, d, kv).wait_recv()
                        dv_own[half, kv] += dv_rcv[half, d - 1, kv].astype(F32)

            for kv in range(2):
                col = (half * 2 + kv) * D
                gv[:, col : col + D] = dv_own[half, kv].astype(BF16)

        code_vt = nt(upv[...], gv[...])
        codes[16:32, 0:T] = code_vt
        code_vt = code_vt.astype(BF16)
        hidden_v = hid[16:32, 0:T].astype(BF16)
        up_v_terms = nn(hidden_v, gv[...])
        for i in range(DP):
            col = D * (i // 4)
            term_v[i, :, 512:640] = up_v_terms[:, col : col + D].astype(BF16)
        down_terms(term_v, code_vt)
        each(lambda off: term_copy(1, off).start())
        rcv_v[0] = term_v[p]

    with jax.named_scope("w_wait"):
        w_load.wait()
        w_arrived(4, *range(13, 20))
        code = (ADAPTER_SCALE * codes[...].astype(BF16).astype(F32)).T
        code = code[0:T, :].astype(BF16)

    def dx_step(i, carry):
        cols = pl.ds(pl.multiple_of(i * SHARD, SHARD), SHARD)
        dx[:, cols] = (nt(gv[...], w[i]) + nn(code, dw[:, cols])).astype(BF16)
        return carry

    with jax.named_scope("dx_1"):
        lax.fori_loop(0, 8, dx_step, 0, unroll=2)

    with jax.named_scope("sum_dp"):
        each(lambda off: term_copy(0, off).wait_recv())
        each(lambda off: term_copy(1, off).wait_recv())
        rs_src[...] = jnp.zeros_like(rs_src)
        sum_q = jnp.sum(rcv_q[...].astype(F32), axis=0)
        sum_v = jnp.sum(rcv_v[...].astype(F32), axis=0)
        for j in range(6):
            rs_src[:, j, :] = sum_q[:, j * D : (j + 1) * D]
        for j in range(5):
            rs_src[:, 6 + j, :] = sum_v[:, j * D : (j + 1) * D]

    def row_copy(off):
        target = lax.rem(c + off, CTX)
        return remote(
            rs_src.at[target], rs_rcv.at[off], r_ssem.at[0, off], r_rsem.at[0, off], target, p
        )

    def sum_copy(off, src=None):
        target = lax.rem(c + off, CTX)
        return remote(ag.at[c], ag.at[c], r_ssem.at[1, off], r_rsem.at[1, off], target, p)

    def sum_arrived(off):
        src = lax.rem(c + CTX - off, CTX)
        remote(ag.at[src], ag.at[src], r_ssem.at[1, off], r_rsem.at[1, off], src, p).wait_recv()

    each(lambda off: row_copy(off).start())
    rs_rcv[0] = rs_src[c]

    with jax.named_scope("dx_2"):
        lax.fori_loop(8, 12, dx_step, 0, unroll=2)

    with jax.named_scope("sum_ctx"):
        each(lambda off: row_copy(off).wait_recv())
        gradient_scale = ADAPTER_SCALE / math.sqrt(DP * CTX * T)
        ag[c] = jnp.sum(rs_rcv[...], axis=0) * gradient_scale
        each(lambda off: sum_copy(off).start())

    with jax.named_scope("dx_3"):
        lax.fori_loop(12, 16, dx_step, 0, unroll=2)

    with jax.named_scope("outputs"):
        each(sum_arrived)
        ag_out[...] = ag[...]

    with jax.named_scope("drain"):
        for kv in range(2):
            kv_copy(first_half, 0, kv).wait_send()

        @pl.when(parity == 0)
        def _():
            for slot in range(3):
                for kv in range(2):
                    kv_copy(second_half, slot, kv).wait_send()

        @pl.when(parity == 1)
        def _():
            for kv in range(2):
                kv_copy(first_half, 1, kv).wait_send()

        for half in range(2):
            for d in range(1, 4):

                @pl.when(lags[half] >= d)
                def _(half=half, d=d):
                    for kv in range(2):
                        dv_copy(half, d, kv).wait_send()

        for number in range(20):
            w_copy(number).wait_send()

        def sent(off):
            term_copy(0, off).wait_send()
            term_copy(1, off).wait_send()
            row_copy(off).wait_send()
            sum_copy(off).wait_send()

        each(sent)


def place(sums, dx, down_q_out, up_q_out, down_v_out, up_v_out, dx_out, wide, narrow, sem):
    p = lax.axis_index("dp")
    copies = [pltpu.make_async_copy(dx, dx_out.at[0], sem.at[0])]
    copies[0].start()
    for j in range(11):
        wide[:, j * D : (j + 1) * D] = sums[:, j, :]
    piece = sums[:, 10, :]
    for j in range(4):

        @pl.when(lax.rem(p, 4) == j)
        def _(j=j):
            narrow[...] = piece[:, 32 * j : 32 * (j + 1)]

    for src, dst in (
        (wide.at[:, 0:512], down_q_out),
        (wide.at[:, 512:768], up_q_out),
        (wide.at[:, 768:1280], down_v_out),
        (narrow, up_v_out),
    ):
        copies.append(pltpu.make_async_copy(src, dst, sem.at[len(copies)]))
        copies[-1].start()
    for copy in copies:
        copy.wait()


def deliver(sums, dx):
    return pl.pallas_call(
        place,
        out_shape=(
            jax.ShapeDtypeStruct((16, SHARD), F32),
            jax.ShapeDtypeStruct((16, DQ // DP), F32),
            jax.ShapeDtypeStruct((16, SHARD), F32),
            jax.ShapeDtypeStruct((16, DKV // DP), F32),
            jax.ShapeDtypeStruct((1, T, WIDTH), BF16),
        ),
        in_specs=[pl.BlockSpec(memory_space=pltpu.VMEM)] * 2,
        out_specs=[pl.BlockSpec(memory_space=pl.ANY)] * 5,
        scratch_shapes=[
            pltpu.VMEM((16, 11 * D), F32),
            pltpu.VMEM((16, DKV // DP), F32),
            pltpu.SemaphoreType.DMA((5,)),
        ],
        compiler_params=pltpu.CompilerParams(vmem_limit_bytes=16 * 1024 * 1024),
    )(
        pltpu.with_memory_space_constraint(sums, pltpu.VMEM),
        pltpu.with_memory_space_constraint(dx, pltpu.VMEM),
    )


def on_device(
    inputs,
    query_saved,
    key_saved,
    value_saved,
    grad_out,
    value_weight,
    query_down_weight,
    up_q,
    value_down_weight,
    up_v,
):
    sums, dx = pl.pallas_call(
        kernel,
        out_shape=(
            pltpu.VMEM((CTX, 16, D), F32),
            pltpu.VMEM((T, WIDTH), BF16),
        ),
        in_specs=[pl.BlockSpec(memory_space=pl.ANY)] * 10,
        out_specs=[pl.BlockSpec(memory_space=pltpu.VMEM)] * 2,
        scratch_shapes=[
            pltpu.VMEM((T, WIDTH), BF16),
            pltpu.VMEM((T, DQ), BF16),
            pltpu.VMEM((T, DQ), BF16),
            pltpu.VMEM((2, 4, 2, 2, T, D), BF16),
            pltpu.VMEM((DP, SHARD, DKV), BF16),
            pltpu.VMEM((32, WIDTH), BF16),
            pltpu.VMEM((16, DQ), BF16),
            pltpu.VMEM((16, DKV), BF16),
            pltpu.VMEM((T, LANES), F32),
            pltpu.VMEM((4 * T, LANES), F32),
            pltpu.VMEM((4 * T, LANES), F32),
            pltpu.VMEM((4 * T, LANES), BF16),
            pltpu.VMEM((4 * T, LANES), BF16),
            pltpu.VMEM((D, 4 * T), BF16),
            pltpu.VMEM((4 * T, D), F32),
            pltpu.VMEM((2, 2, T, D), F32),
            pltpu.VMEM((2, 3, 2, T, D), BF16),
            pltpu.VMEM((2, 3, 2, T, D), BF16),
            pltpu.VMEM((QUADS, D, LANES), BF16),
            pltpu.VMEM((T, DKV), BF16),
            pltpu.VMEM((32, 256), F32),
            pltpu.VMEM((64, LANES), BF16),
            pltpu.VMEM((32, 256), F32),
            pltpu.VMEM((DP, 16, 768), BF16),
            pltpu.VMEM((DP, 16, 640), BF16),
            pltpu.VMEM((DP, 16, 768), BF16),
            pltpu.VMEM((DP, 16, 640), BF16),
            pltpu.VMEM((CTX, 16, D), F32),
            pltpu.VMEM((CTX, 16, D), F32),
            pltpu.VMEM((CTX, 16, D), F32),
            pltpu.SemaphoreType.DMA((16,)),
            pltpu.SemaphoreType.DMA((2, 4, 2)),
            pltpu.SemaphoreType.DMA((2, 4, 2)),
            pltpu.SemaphoreType.DMA((20,)),
            pltpu.SemaphoreType.DMA((20,)),
            pltpu.SemaphoreType.DMA((2, 3, 2)),
            pltpu.SemaphoreType.DMA((2, 3, 2)),
            pltpu.SemaphoreType.DMA((2, 16)),
            pltpu.SemaphoreType.DMA((2, 16)),
            pltpu.SemaphoreType.DMA((2, 16)),
            pltpu.SemaphoreType.DMA((2, 16)),
        ],
        compiler_params=pltpu.CompilerParams(
            collective_id=0, has_side_effects=True, vmem_limit_bytes=44 * 1024 * 1024
        ),
    )(
        *(
            pltpu.with_memory_space_constraint(operand, pltpu.HBM)
            for operand in (
                inputs[0],
                query_saved[0],
                key_saved[0],
                value_saved[0],
                grad_out[0],
                value_weight,
                query_down_weight,
                up_q,
                value_down_weight,
                up_v,
            )
        )
    )
    return deliver(sums, dx)


def solution(mesh):
    in_specs = (
        P("dp", "ctx", None),
        P("dp", "ctx", None),
        P("dp", "ctx", None),
        P("dp", "ctx", None),
        P("dp", "ctx", None),
        P("dp", None),
        P(),
        P(),
        P(),
        P(),
    )
    out_specs = (P(None, "dp"), P(None, "dp"), P(None, "dp"), P(None, "dp"), P("dp", "ctx", None))
    return jax.shard_map(
        on_device, mesh=mesh, in_specs=in_specs, out_specs=out_specs, check_vma=False
    )
```

```python
import functools
import math

import jax
import jax.numpy as jnp
from jax import lax
from jax.experimental import pallas as pl
from jax.experimental.pallas import tpu as pltpu
from jax.sharding import PartitionSpec as P

MESH = pl.DeviceIdType.MESH
F32 = jnp.float32
BF16 = jnp.bfloat16

CTX = 16
DP = 16
T = 192
D = 128
LANES = 4 * T
QUADS = 8
WIDTH = 8192
SHARD = WIDTH // DP
DQ = 4096
DKV = 512
ADAPTER_SCALE = 2.0
CHUNK = 32


def nt(a, b):
    return lax.dot_general(a, b, (((1,), (1,)), ((), ())), preferred_element_type=F32)


def nn(a, b):
    return jnp.dot(a, b, preferred_element_type=F32)


def kernel(
    x_hbm,
    q_hbm,
    k_hbm,
    v_hbm,
    g_hbm,
    w_hbm,
    qdw_hbm,
    upq_hbm,
    vdw_hbm,
    upv_hbm,
    ag_out,
    dx,
    x,
    q,
    g,
    kvw,
    w,
    dw,
    upq,
    upv,
    bias,
    s_buf,
    dp_buf,
    pb_buf,
    ds_buf,
    kt,
    dv_acc,
    dv_own,
    dv_snd,
    dv_rcv,
    gq,
    gv,
    hid,
    ht4,
    codes,
    term_q,
    term_v,
    rcv_q,
    rcv_v,
    rs_src,
    rs_rcv,
    ag,
    loc_sem,
    kv_ssem,
    kv_rsem,
    w_ssem,
    w_rsem,
    dv_ssem,
    dv_rsem,
    t_ssem,
    t_rsem,
    r_ssem,
    r_rsem,
):
    c = lax.axis_index("ctx")
    p = lax.axis_index("dp")
    right = lax.rem(c + 1, CTX)
    scale = 1.0 / math.sqrt(D)
    exp2_scale = scale * math.log2(math.e)

    def remote(src, dst, ssem, rsem, ctx, dp):
        return pltpu.make_async_remote_copy(
            src_ref=src,
            dst_ref=dst,
            send_sem=ssem,
            recv_sem=rsem,
            device_id=(ctx, dp),
            device_id_type=MESH,
        )

    loads = []

    def load(src, dst):
        copy = pltpu.make_async_copy(src, dst, loc_sem.at[len(loads)])
        copy.start()
        loads.append(copy)
        return copy

    kv_loads = []
    for half in range(2):
        for which, ref in ((0, k_hbm), (1, v_hbm)):
            for head in range(2):
                col = (half * 2 + head) * D
                kv_loads.append(load(ref.at[:, col : col + D], kvw.at[half, 0, head, which]))
    dw_loads = [load(qdw_hbm, dw.at[0:16]), load(vdw_hbm, dw.at[16:32])]
    x_load = load(x_hbm, x)
    q_load = load(q_hbm, q)
    g_load = load(g_hbm, g)
    up_loads = [load(upq_hbm, upq), load(upv_hbm, upv)]
    w_load = load(w_hbm, w.at[p])

    with jax.named_scope("greet"):
        barrier = pltpu.get_barrier_semaphore()

        def greet(off, carry):
            pl.semaphore_signal(
                barrier, inc=1, device_id=(lax.rem(c + off, CTX), p), device_id_type=MESH
            )
            pl.semaphore_signal(
                barrier, inc=1, device_id=(c, lax.rem(p + off, DP)), device_id_type=MESH
            )
            return carry

        lax.fori_loop(1, 16, greet, 0, unroll=True)
        pl.semaphore_signal(
            barrier,
            inc=1,
            device_id=(lax.rem(c + 8, CTX), lax.rem(p + 8, DP)),
            device_id_type=MESH,
        )
        pl.semaphore_wait(barrier, 31)

    lags = (lax.rem(c, 4), lax.rem(c + 2, 4))
    parity = lax.rem(c, 2)
    first_half = lax.rem(c, 4) // 2
    second_half = 1 - first_half

    def kv_copy(half, slot, kv):
        return remote(
            kvw.at[half, slot, kv],
            kvw.at[half, slot + 1, kv],
            kv_ssem.at[half, slot, kv],
            kv_rsem.at[half, slot + 1, kv],
            right,
            p,
        )

    def kv_arrived(half, slot, kv):
        remote(
            kvw.at[half, slot, kv],
            kvw.at[half, slot, kv],
            kv_ssem.at[half, slot, kv],
            kv_rsem.at[half, slot, kv],
            right,
            p,
        ).wait_recv()

    with jax.named_scope("kv_send"):
        for copy in kv_loads:
            copy.wait()
        for kv in range(2):
            kv_copy(first_half, 0, kv).start()

    core = lax.rem(p, 2)
    px = lax.rem(p // 2, 4)
    py = p // 8

    def at(dy, dx_, dc):
        yy = lax.rem(py + dy, 2)
        xx = lax.rem(px + dx_ + 4, 4)
        cc = lax.rem(core + dc, 2)
        return yy * 8 + xx * 2 + cc

    x_up, x_dn, y_nb, sib = at(0, 1, 0), at(0, -1, 0), at(1, 0, 0), at(0, 0, 1)
    far = lax.rem(c + 8, CTX)
    rows = SHARD // 2
    own, up, dn, opp = p, x_up, x_dn, at(0, 2, 0)
    y_own, y_up, y_dn, y_opp = at(1, 0, 0), at(1, 1, 0), at(1, -1, 0), at(1, 2, 0)
    w_plan = [
        (own, dn, 2, c, x_up),
        (own, up, 2, c, x_dn),
        (own, y_own, 0, c, y_nb),
        (own, y_own, 1, far, y_nb),
        (own, sib, 2, c, sib),
        (up, opp, 0, c, x_dn),
        (dn, opp, 1, c, x_up),
        (up, y_up, 0, c, y_nb),
        (dn, y_dn, 0, far, y_nb),
        (y_own, y_up, 1, c, x_dn),
        (y_own, y_dn, 1, c, x_up),
        (opp, y_opp, 0, c, y_nb),
        (opp, y_opp, 1, far, y_nb),
        (dn, at(0, -1, 1), 2, c, sib),
        (up, at(0, 1, 1), 2, c, sib),
        (y_own, at(1, 0, 1), 2, c, sib),
        (opp, at(0, 2, 1), 2, c, sib),
        (y_up, at(1, 1, 1), 2, c, sib),
        (y_dn, at(1, -1, 1), 2, c, sib),
        (y_opp, at(1, 2, 1), 2, c, sib),
    ]

    def w_part(shard, part):
        return w.at[shard] if part == 2 else w.at[shard, part * rows : (part + 1) * rows]

    def w_copy(number):
        shard, _, part, ctx, target = w_plan[number]
        block = w_part(shard, part)
        src = block
        if number < 5:
            src = w_hbm if part == 2 else w_hbm.at[part * rows : (part + 1) * rows]
        return remote(src, block, w_ssem.at[number], w_rsem.at[number], ctx, target)

    def w_arrived(*numbers):
        for number in numbers:
            _, shard, part, ctx, target = w_plan[number]
            block = w_part(shard, part)
            remote(
                block, block, w_ssem.at[number], w_rsem.at[number], ctx, target
            ).wait_recv()

    def w_start(*numbers):
        for number in numbers:
            w_copy(number).start()

    def w_round_1():
        with jax.named_scope("w_round_1"):
            w_arrived(0, 1, 2, 3)
            w_start(5, 6, 7, 8, 9, 10, 13, 14, 15)

    def w_round_2():
        with jax.named_scope("w_round_2"):
            w_arrived(5, 6)
            w_start(11, 12, 16)

    w_start(2, 3, 0, 1, 4)

    with jax.named_scope("bias"):
        row = lax.broadcasted_iota(jnp.int32, (T, LANES), 0)
        lane = lax.broadcasted_iota(jnp.int32, (T, LANES), 1)
        turn = (
            (lane >= T).astype(jnp.int32)
            + (lane >= 2 * T).astype(jnp.int32)
            + (lane >= 3 * T).astype(jnp.int32)
        )
        bias[...] = jnp.where(row <= lane - turn * T, 0.0, -jnp.inf).astype(F32)

    with jax.named_scope("hidden"):
        for copy in dw_loads:
            copy.wait()
        x_load.wait()

        def hidden_step(i, acc):
            cols = pl.ds(pl.multiple_of(i * 1024, 1024), 1024)
            return acc + nt(dw[:, cols], x[:, cols])

        hidden = lax.fori_loop(0, 8, hidden_step, jnp.zeros((32, T), F32))
        hid[...] = jnp.zeros_like(hid)
        hid[:, 0:T] = hidden.astype(BF16).astype(F32)
        ht4[...] = jnp.zeros_like(ht4)
        padded = hid[0:16, :]
        turned = pltpu.roll(padded, 64, 1)
        ht4[0:16, 0:256] = padded.astype(BF16)
        ht4[16:32, 128:384] = turned.astype(BF16)
        ht4[32:48, 384:640] = padded.astype(BF16)
        ht4[48:64, 512:768] = turned.astype(BF16)

    q_load.wait()
    g_load.wait()

    def four_heads(ref, quad):
        block = ref[:, pl.ds(pl.multiple_of(quad * 512, 512), 512)]
        return jnp.concatenate([block[:, i * D : (i + 1) * D] for i in range(4)], axis=0)

    def attend(half, kv, nk, between=None):
        n = nk * T
        keys = kvw[half, 0:nk, kv, 0].reshape(n, D)
        kt[:, 0:n] = keys.T
        quads = [half * 4 + kv * 2 + i for i in range(2)]
        tops, invs, deltas = {}, {}, {}

        def scores(i):
            q4 = four_heads(q, quads[i])
            top = None
            for d in range(nk):
                s = nt(kvw[half, d, kv, 0], q4)
                if d == 0:
                    s = s + bias[...]
                s_buf[i, d * T : (d + 1) * T] = s
                m = jnp.max(s, axis=0, keepdims=True)
                top = m if top is None else jnp.maximum(top, m)
            tops[i] = top

        def values(i):
            g4 = four_heads(g, quads[i])
            for d in range(nk):
                dp_buf[i, d * T : (d + 1) * T] = nt(kvw[half, d, kv, 1], g4)

        def weigh(i):
            values(i)
            top = tops[i]

            def exp_step(j, sums):
                rows = pl.ds(pl.multiple_of(j * CHUNK, CHUNK), CHUNK)
                e = jnp.exp2((s_buf[i, rows] - top) * exp2_scale)
                s_buf[i, rows] = e
                return (
                    sums[0] + jnp.sum(e.reshape(CHUNK // 8, 8, LANES), axis=0),
                    sums[1]
                    + jnp.sum((e * dp_buf[i, rows]).reshape(CHUNK // 8, 8, LANES), axis=0),
                )

            zero = jnp.zeros((8, LANES), F32)
            total, weighted = lax.fori_loop(0, n // CHUNK, exp_step, (zero, zero), unroll=True)
            invs[i] = 1.0 / jnp.sum(total, axis=0, keepdims=True)
            deltas[i] = jnp.sum(weighted, axis=0, keepdims=True) * invs[i]

        def grads(i):
            inv, delta = invs[i], deltas[i]

            def grad_step(j, carry):
                rows = pl.ds(pl.multiple_of(j * CHUNK, CHUNK), CHUNK)
                probs = s_buf[i, rows] * inv
                pb_buf[i, rows] = probs.astype(BF16)
                ds_buf[i, rows] = (probs * (dp_buf[i, rows] - delta)).astype(BF16)
                return carry

            lax.fori_loop(0, n // CHUNK, grad_step, 0, unroll=True)

        def products(i):
            g4 = four_heads(g, quads[i])
            dv = nn(pb_buf[i, 0:n], g4)
            if i == 0:
                dv_acc[0:n] = dv
            else:
                dv_acc[0:n] += dv
            gq[quads[i]] = (nn(kt[:, 0:n], ds_buf[i, 0:n]) * scale).astype(BF16)

        for i in range(2):
            scores(i)
            if i == 0 and between is not None:
                between()
            weigh(i)
            grads(i)
            products(i)
        dv_own[half, kv] = dv_acc[0:T]
        for d in range(1, nk):
            dv_snd[half, d - 1, kv] = dv_acc[d * T : (d + 1) * T].astype(BF16)
            dv_copy(half, d, kv).start()

    def dv_copy(half, d, kv):
        return remote(
            dv_snd.at[half, d - 1, kv],
            dv_rcv.at[half, d - 1, kv],
            dv_ssem.at[half, d - 1, kv],
            dv_rsem.at[half, d - 1, kv],
            lax.rem(c + CTX - d, CTX),
            p,
        )

    @pl.when(parity == 0)
    def _():
        def first_step(kv, carry):
            attend(first_half, kv, 1)

            @pl.when(kv == 0)
            def _():
                kv_copy(second_half, 0, 0).start()

            return carry

        with jax.named_scope("even_first"):
            lax.fori_loop(0, 2, first_step, 0)
        with jax.named_scope("even_pass"):
            kv_arrived(second_half, 1, 0)
            kv_copy(second_half, 1, 0).start()
            kv_arrived(second_half, 2, 0)
            kv_copy(second_half, 2, 0).start()
            kv_copy(second_half, 0, 1).start()
            kv_arrived(second_half, 1, 1)
            kv_copy(second_half, 1, 1).start()

        def second_step(kv, carry):
            @pl.when(kv == 1)
            def _():
                kv_arrived(second_half, 2, 1)
                kv_copy(second_half, 2, 1).start()
                w_round_1()

            attend(second_half, kv, 3)
            return carry

        with jax.named_scope("even_second"):
            lax.fori_loop(0, 2, second_step, 0)

    @pl.when(parity == 1)
    def _():
        def first_step(kv, carry):
            kv_arrived(first_half, 1, kv)
            kv_copy(first_half, 1, kv).start()
            attend(first_half, kv, 2)
            return carry

        with jax.named_scope("odd_first"):
            lax.fori_loop(0, 2, first_step, 0)

        def second_step(kv, carry):
            for slot in (1, 2, 3):
                kv_arrived(second_half, slot, kv)

            def between():
                pl.when(kv == 0)(w_round_1)

            attend(second_half, kv, 4, between)
            return carry

        with jax.named_scope("odd_second"):
            lax.fori_loop(0, 2, second_step, 0)

    with jax.named_scope("query_terms"):
        for copy in up_loads:
            copy.wait()
        flat_gq = gq[...].reshape(QUADS * D, LANES)
        up4 = jnp.concatenate(
            [
                jnp.concatenate(
                    [upq[:, (4 * i + j) * D : (4 * i + j + 1) * D] for i in range(QUADS)], axis=1
                )
                for j in range(4)
            ],
            axis=0,
        )
        r = nn(up4, flat_gq)
        code_q = (
            r[0:16, 0:256]
            + pltpu.roll(r[16:32, 128:384], 192, 1)
            + r[32:48, 384:640]
            + pltpu.roll(r[48:64, 512:768], 192, 1)
        )
        codes[...] = jnp.zeros_like(codes)
        codes[0:16, :] = code_q
        code_qt = codes[0:16, 0:T].astype(BF16)
        up_terms = nt(ht4[...], flat_gq)
        for i in range(DP):
            lo = 32 * (i % 2)
            col = D * (i // 2)
            term_q[i, :, 512:640] = up_terms[lo : lo + 16, col : col + D].astype(BF16)
            term_q[i, :, 640:768] = up_terms[lo + 16 : lo + 32, col : col + D].astype(BF16)

    def down_terms(term, code):
        def step(i, carry):
            cols = pl.ds(pl.multiple_of(i * SHARD, SHARD), SHARD)
            term[i, :, 0:SHARD] = nn(code, x[:, cols]).astype(BF16)
            return carry

        lax.fori_loop(0, DP, step, 0, unroll=4)

    def term_copy(which, off):
        target = lax.rem(p + off, DP)
        term, rcv = ((term_q, rcv_q), (term_v, rcv_v))[which]
        return remote(
            term.at[target],
            rcv.at[off],
            t_ssem.at[which, off],
            t_rsem.at[which, off],
            c,
            target,
        )

    def each(fn):
        def step(off, carry):
            fn(off)
            return carry

        lax.fori_loop(1, 16, step, 0, unroll=True)

    with jax.named_scope("query_down"):
        down_terms(term_q, code_qt)
        each(lambda off: term_copy(0, off).start())
        rcv_q[0] = term_q[p]

    w_round_2()

    with jax.named_scope("value_gradient"):
        for half in range(2):
            for d in range(1, 4):

                @pl.when(lags[half] + d <= 3)
                def _(half=half, d=d):
                    for kv in range(2):
                        dv_copy(half, d, kv).wait_recv()
                        dv_own[half, kv] += dv_rcv[half, d - 1, kv].astype(F32)

            for kv in range(2):
                col = (half * 2 + kv) * D
                gv[:, col : col + D] = dv_own[half, kv].astype(BF16)

        code_vt = nt(upv[...], gv[...])
        codes[16:32, 0:T] = code_vt
        code_vt = code_vt.astype(BF16)
        hidden_v = hid[16:32, 0:T].astype(BF16)
        up_v_terms = nn(hidden_v, gv[...])
        for i in range(DP):
            col = D * (i // 4)
            term_v[i, :, 512:640] = up_v_terms[:, col : col + D].astype(BF16)
        down_terms(term_v, code_vt)
        each(lambda off: term_copy(1, off).start())
        rcv_v[0] = term_v[p]

    with jax.named_scope("w_round_3"):
        w_arrived(7, 8, 9, 10)
        w_start(17, 18)

    def input_gradient():
        w_load.wait()
        w_arrived(4, *range(13, 20))
        code = (ADAPTER_SCALE * codes[...].astype(BF16).astype(F32)).T
        code = code[0:T, :].astype(BF16)

        def step(i, carry):
            cols = pl.ds(pl.multiple_of(i * SHARD, SHARD), SHARD)
            dx[:, cols] = (nt(gv[...], w[i]) + nn(code, dw[:, cols])).astype(BF16)
            return carry

        lax.fori_loop(0, DP, step, 0, unroll=2)

    with jax.named_scope("sum_dp"):
        each(lambda off: term_copy(0, off).wait_recv())
        sum_q = jnp.sum(rcv_q[...].astype(F32), axis=0)
        rs_src[...] = jnp.zeros_like(rs_src)
        for j in range(6):
            rs_src[:, j, :] = sum_q[:, j * D : (j + 1) * D]
        each(lambda off: term_copy(1, off).wait_recv())
        sum_v = jnp.sum(rcv_v[...].astype(F32), axis=0)
        for j in range(5):
            rs_src[:, 6 + j, :] = sum_v[:, j * D : (j + 1) * D]

    def row_copy(off):
        target = lax.rem(c + off, CTX)
        return remote(
            rs_src.at[target], rs_rcv.at[off], r_ssem.at[0, off], r_rsem.at[0, off], target, p
        )

    def sum_copy(off):
        target = lax.rem(c + off, CTX)
        return remote(ag.at[c], ag.at[c], r_ssem.at[1, off], r_rsem.at[1, off], target, p)

    def sum_arrived(off):
        src = lax.rem(c + CTX - off, CTX)
        remote(ag.at[src], ag.at[src], r_ssem.at[1, off], r_rsem.at[1, off], src, p).wait_recv()

    each(lambda off: row_copy(off).start())
    rs_rcv[0] = rs_src[c]
    w_arrived(11, 12)
    w_start(19)

    z = lax.rem(c, 8)
    early = (z <= 2) | (z >= 6)
    with jax.named_scope("dx_early"):
        pl.when(early)(input_gradient)
    with jax.named_scope("sum_ctx"):
        each(lambda off: row_copy(off).wait_recv())
        gradient_scale = ADAPTER_SCALE / math.sqrt(DP * CTX * T)
        ag[c] = jnp.sum(rs_rcv[...], axis=0) * gradient_scale
        each(lambda off: sum_copy(off).start())
    with jax.named_scope("dx_late"):
        pl.when(jnp.logical_not(early))(input_gradient)
    with jax.named_scope("outputs"):
        each(sum_arrived)
        ag_out[...] = ag[...]

    with jax.named_scope("drain"):
        for kv in range(2):
            kv_copy(first_half, 0, kv).wait_send()

        @pl.when(parity == 0)
        def _():
            for slot in range(3):
                for kv in range(2):
                    kv_copy(second_half, slot, kv).wait_send()

        @pl.when(parity == 1)
        def _():
            for kv in range(2):
                kv_copy(first_half, 1, kv).wait_send()

        for half in range(2):
            for d in range(1, 4):

                @pl.when(lags[half] >= d)
                def _(half=half, d=d):
                    for kv in range(2):
                        dv_copy(half, d, kv).wait_send()

        for number in range(20):
            w_copy(number).wait_send()

        def sent(off):
            term_copy(0, off).wait_send()
            term_copy(1, off).wait_send()
            row_copy(off).wait_send()
            sum_copy(off).wait_send()

        each(sent)


def place(sums, dx, down_q_out, up_q_out, down_v_out, up_v_out, dx_out, wide, narrow, sem):
    p = lax.axis_index("dp")
    copies = [pltpu.make_async_copy(dx, dx_out.at[0], sem.at[0])]
    copies[0].start()
    for j in range(11):
        wide[:, j * D : (j + 1) * D] = sums[:, j, :]
    piece = sums[:, 10, :]
    for j in range(4):

        @pl.when(lax.rem(p, 4) == j)
        def _(j=j):
            narrow[...] = piece[:, 32 * j : 32 * (j + 1)]

    for src, dst in (
        (wide.at[:, 0:512], down_q_out),
        (wide.at[:, 512:768], up_q_out),
        (wide.at[:, 768:1280], down_v_out),
        (narrow, up_v_out),
    ):
        copies.append(pltpu.make_async_copy(src, dst, sem.at[len(copies)]))
        copies[-1].start()
    for copy in copies:
        copy.wait()


def deliver(sums, dx):
    return pl.pallas_call(
        place,
        out_shape=(
            jax.ShapeDtypeStruct((16, SHARD), F32),
            jax.ShapeDtypeStruct((16, DQ // DP), F32),
            jax.ShapeDtypeStruct((16, SHARD), F32),
            jax.ShapeDtypeStruct((16, DKV // DP), F32),
            jax.ShapeDtypeStruct((1, T, WIDTH), BF16),
        ),
        in_specs=[pl.BlockSpec(memory_space=pltpu.VMEM)] * 2,
        out_specs=[pl.BlockSpec(memory_space=pl.ANY)] * 5,
        scratch_shapes=[
            pltpu.VMEM((16, 11 * D), F32),
            pltpu.VMEM((16, DKV // DP), F32),
            pltpu.SemaphoreType.DMA((5,)),
        ],
        compiler_params=pltpu.CompilerParams(vmem_limit_bytes=16 * 1024 * 1024),
    )(
        pltpu.with_memory_space_constraint(sums, pltpu.VMEM),
        pltpu.with_memory_space_constraint(dx, pltpu.VMEM),
    )


def on_device(
    inputs,
    query_saved,
    key_saved,
    value_saved,
    grad_out,
    value_weight,
    query_down_weight,
    up_q,
    value_down_weight,
    up_v,
):
    sums, dx = pl.pallas_call(
        kernel,
        out_shape=(
            pltpu.VMEM((CTX, 16, D), F32),
            pltpu.VMEM((T, WIDTH), BF16),
        ),
        in_specs=[pl.BlockSpec(memory_space=pl.ANY)] * 10,
        out_specs=[pl.BlockSpec(memory_space=pltpu.VMEM)] * 2,
        scratch_shapes=[
            pltpu.VMEM((T, WIDTH), BF16),
            pltpu.VMEM((T, DQ), BF16),
            pltpu.VMEM((T, DQ), BF16),
            pltpu.VMEM((2, 4, 2, 2, T, D), BF16),
            pltpu.VMEM((DP, SHARD, DKV), BF16),
            pltpu.VMEM((32, WIDTH), BF16),
            pltpu.VMEM((16, DQ), BF16),
            pltpu.VMEM((16, DKV), BF16),
            pltpu.VMEM((T, LANES), F32),
            pltpu.VMEM((2, 4 * T, LANES), F32),
            pltpu.VMEM((2, 4 * T, LANES), F32),
            pltpu.VMEM((2, 4 * T, LANES), BF16),
            pltpu.VMEM((2, 4 * T, LANES), BF16),
            pltpu.VMEM((D, 4 * T), BF16),
            pltpu.VMEM((4 * T, D), F32),
            pltpu.VMEM((2, 2, T, D), F32),
            pltpu.VMEM((2, 3, 2, T, D), BF16),
            pltpu.VMEM((2, 3, 2, T, D), BF16),
            pltpu.VMEM((QUADS, D, LANES), BF16),
            pltpu.VMEM((T, DKV), BF16),
            pltpu.VMEM((32, 256), F32),
            pltpu.VMEM((64, LANES), BF16),
            pltpu.VMEM((32, 256), F32),
            pltpu.VMEM((DP, 16, 768), BF16),
            pltpu.VMEM((DP, 16, 640), BF16),
            pltpu.VMEM((DP, 16, 768), BF16),
            pltpu.VMEM((DP, 16, 640), BF16),
            pltpu.VMEM((CTX, 16, D), F32),
            pltpu.VMEM((CTX, 16, D), F32),
            pltpu.VMEM((CTX, 16, D), F32),
            pltpu.SemaphoreType.DMA((16,)),
            pltpu.SemaphoreType.DMA((2, 4, 2)),
            pltpu.SemaphoreType.DMA((2, 4, 2)),
            pltpu.SemaphoreType.DMA((20,)),
            pltpu.SemaphoreType.DMA((20,)),
            pltpu.SemaphoreType.DMA((2, 3, 2)),
            pltpu.SemaphoreType.DMA((2, 3, 2)),
            pltpu.SemaphoreType.DMA((2, 16)),
            pltpu.SemaphoreType.DMA((2, 16)),
            pltpu.SemaphoreType.DMA((2, 16)),
            pltpu.SemaphoreType.DMA((2, 16)),
        ],
        compiler_params=pltpu.CompilerParams(
            collective_id=0, has_side_effects=True, vmem_limit_bytes=52 * 1024 * 1024
        ),
    )(
        *(
            pltpu.with_memory_space_constraint(operand, pltpu.HBM)
            for operand in (
                inputs[0],
                query_saved[0],
                key_saved[0],
                value_saved[0],
                grad_out[0],
                value_weight,
                query_down_weight,
                up_q,
                value_down_weight,
                up_v,
            )
        )
    )
    return deliver(sums, dx)


def solution(mesh):
    in_specs = (
        P("dp", "ctx", None),
        P("dp", "ctx", None),
        P("dp", "ctx", None),
        P("dp", "ctx", None),
        P("dp", "ctx", None),
        P("dp", None),
        P(),
        P(),
        P(),
        P(),
    )
    out_specs = (P(None, "dp"), P(None, "dp"), P(None, "dp"), P(None, "dp"), P("dp", "ctx", None))
    return jax.shard_map(
        on_device, mesh=mesh, in_specs=in_specs, out_specs=out_specs, check_vma=False
    )
```

```python
import functools
import math

import jax
import jax.numpy as jnp
from jax import lax
from jax.experimental import pallas as pl
from jax.experimental.pallas import tpu as pltpu
from jax.sharding import PartitionSpec as P

MESH = pl.DeviceIdType.MESH
F32 = jnp.float32
BF16 = jnp.bfloat16

CTX = 16
DP = 16
T = 192
D = 128
LANES = 4 * T
QUADS = 8
WIDTH = 8192
SHARD = WIDTH // DP
DQ = 4096
DKV = 512
ADAPTER_SCALE = 2.0
CHUNK = 32
FAR_FIRST = (4, 12, 3, 5, 11, 13, 2, 6, 10, 14, 1, 7, 9, 15, 8)


def nt(a, b):
    return lax.dot_general(a, b, (((1,), (1,)), ((), ())), preferred_element_type=F32)


def nn(a, b):
    return jnp.dot(a, b, preferred_element_type=F32)


def kernel(
    x_hbm,
    q_hbm,
    k_hbm,
    v_hbm,
    g_hbm,
    w_hbm,
    qdw_hbm,
    upq_hbm,
    vdw_hbm,
    upv_hbm,
    ag_out,
    dx,
    x,
    q,
    g,
    kvw,
    w,
    dw,
    upq,
    upv,
    bias,
    s_buf,
    dp_buf,
    pb_buf,
    ds_buf,
    kt,
    dv_acc,
    dv_own,
    dv_snd,
    dv_rcv,
    gq,
    gv,
    hid,
    ht4,
    codes,
    term_q,
    term_v,
    rcv_q,
    rcv_v,
    rs_src,
    rs_rcv,
    ag,
    loc_sem,
    kv_ssem,
    kv_rsem,
    w_ssem,
    w_rsem,
    dv_ssem,
    dv_rsem,
    t_ssem,
    t_rsem,
    r_ssem,
    r_rsem,
):
    c = lax.axis_index("ctx")
    p = lax.axis_index("dp")
    right = lax.rem(c + 1, CTX)
    scale = 1.0 / math.sqrt(D)
    exp2_scale = scale * math.log2(math.e)

    def remote(src, dst, ssem, rsem, ctx, dp):
        return pltpu.make_async_remote_copy(
            src_ref=src,
            dst_ref=dst,
            send_sem=ssem,
            recv_sem=rsem,
            device_id=(ctx, dp),
            device_id_type=MESH,
        )

    loads = []

    def load(src, dst):
        copy = pltpu.make_async_copy(src, dst, loc_sem.at[len(loads)])
        copy.start()
        loads.append(copy)
        return copy

    kv_loads = []
    for half in range(2):
        for which, ref in ((0, k_hbm), (1, v_hbm)):
            for head in range(2):
                col = (half * 2 + head) * D
                kv_loads.append(load(ref.at[:, col : col + D], kvw.at[half, 0, head, which]))
    with jax.named_scope("greet"):
        barrier = pltpu.get_barrier_semaphore()

        def greet(off, carry):
            pl.semaphore_signal(
                barrier, inc=1, device_id=(lax.rem(c + off, CTX), p), device_id_type=MESH
            )
            pl.semaphore_signal(
                barrier, inc=1, device_id=(c, lax.rem(p + off, DP)), device_id_type=MESH
            )
            return carry

        lax.fori_loop(1, 16, greet, 0, unroll=True)
        pl.semaphore_signal(
            barrier,
            inc=1,
            device_id=(lax.rem(c + 8, CTX), lax.rem(p + 8, DP)),
            device_id_type=MESH,
        )
        q_load = load(q_hbm, q)
        g_load = load(g_hbm, g)
        dw_loads = [load(qdw_hbm, dw.at[0:16]), load(vdw_hbm, dw.at[16:32])]
        x_load = load(x_hbm, x)
        up_loads = [load(upq_hbm, upq), load(upv_hbm, upv)]
        w_load = load(w_hbm, w.at[p])
        pl.semaphore_wait(barrier, 31)

    lags = (lax.rem(c, 4), lax.rem(c + 2, 4))
    parity = lax.rem(c, 2)
    first_half = lax.rem(c, 4) // 2
    second_half = 1 - first_half

    def kv_copy(half, slot, kv):
        return remote(
            kvw.at[half, slot, kv],
            kvw.at[half, slot + 1, kv],
            kv_ssem.at[half, slot, kv],
            kv_rsem.at[half, slot + 1, kv],
            right,
            p,
        )

    def kv_arrived(half, slot, kv):
        remote(
            kvw.at[half, slot, kv],
            kvw.at[half, slot, kv],
            kv_ssem.at[half, slot, kv],
            kv_rsem.at[half, slot, kv],
            right,
            p,
        ).wait_recv()

    with jax.named_scope("kv_send"):
        for copy in kv_loads:
            copy.wait()
        for kv in range(2):
            kv_copy(first_half, 0, kv).start()

        @pl.when(parity == 0)
        def _():
            kv_copy(second_half, 0, 0).start()

    core = lax.rem(p, 2)
    px = lax.rem(p // 2, 4)
    py = p // 8

    def at(dy, dx_, dc):
        yy = lax.rem(py + dy, 2)
        xx = lax.rem(px + dx_ + 4, 4)
        cc = lax.rem(core + dc, 2)
        return yy * 8 + xx * 2 + cc

    x_up, x_dn, y_nb, sib = at(0, 1, 0), at(0, -1, 0), at(1, 0, 0), at(0, 0, 1)
    far = lax.rem(c + 8, CTX)
    rows = SHARD // 2
    own, up, dn, opp = p, x_up, x_dn, at(0, 2, 0)
    y_own, y_up, y_dn, y_opp = at(1, 0, 0), at(1, 1, 0), at(1, -1, 0), at(1, 2, 0)
    w_plan = [
        (own, dn, 2, c, x_up),
        (own, up, 2, c, x_dn),
        (own, y_own, 0, c, y_nb),
        (own, y_own, 1, far, y_nb),
        (own, sib, 2, c, sib),
        (up, opp, 0, c, x_dn),
        (dn, opp, 1, c, x_up),
        (up, y_up, 0, c, y_nb),
        (dn, y_dn, 0, far, y_nb),
        (y_own, y_up, 1, c, x_dn),
        (y_own, y_dn, 1, c, x_up),
        (opp, y_opp, 0, c, y_nb),
        (opp, y_opp, 1, far, y_nb),
        (dn, at(0, -1, 1), 2, c, sib),
        (up, at(0, 1, 1), 2, c, sib),
        (y_own, at(1, 0, 1), 2, c, sib),
        (opp, at(0, 2, 1), 2, c, sib),
        (y_up, at(1, 1, 1), 2, c, sib),
        (y_dn, at(1, -1, 1), 2, c, sib),
        (y_opp, at(1, 2, 1), 2, c, sib),
    ]

    def w_part(shard, part):
        return w.at[shard] if part == 2 else w.at[shard, part * rows : (part + 1) * rows]

    def w_copy(number):
        shard, _, part, ctx, target = w_plan[number]
        block = w_part(shard, part)
        src = block
        if number < 5:
            src = w_hbm if part == 2 else w_hbm.at[part * rows : (part + 1) * rows]
        return remote(src, block, w_ssem.at[number], w_rsem.at[number], ctx, target)

    def w_arrived(*numbers):
        for number in numbers:
            _, shard, part, ctx, target = w_plan[number]
            block = w_part(shard, part)
            remote(
                block, block, w_ssem.at[number], w_rsem.at[number], ctx, target
            ).wait_recv()

    def w_start(*numbers):
        for number in numbers:
            w_copy(number).start()

    def w_round_1():
        with jax.named_scope("w_round_1"):
            w_arrived(0, 1, 2, 3)
            w_start(5, 6, 7, 8, 9, 10, 13, 14, 15)

    def w_round_2():
        with jax.named_scope("w_round_2"):
            w_arrived(5, 6)
            w_start(11, 12, 16)

    w_start(2, 3, 0, 1, 4)

    with jax.named_scope("bias"):
        row = lax.broadcasted_iota(jnp.int32, (T, LANES), 0)
        lane = lax.broadcasted_iota(jnp.int32, (T, LANES), 1)
        turn = (
            (lane >= T).astype(jnp.int32)
            + (lane >= 2 * T).astype(jnp.int32)
            + (lane >= 3 * T).astype(jnp.int32)
        )
        bias[...] = jnp.where(row <= lane - turn * T, 0.0, -jnp.inf).astype(F32)

    @pl.when(parity == 0)
    def _():
        kv_arrived(second_half, 1, 0)
        kv_copy(second_half, 1, 0).start()

    q_load.wait()
    g_load.wait()

    def four_heads(ref, quad):
        block = ref[:, pl.ds(pl.multiple_of(quad * 512, 512), 512)]
        return jnp.concatenate([block[:, i * D : (i + 1) * D] for i in range(4)], axis=0)

    def attend(half, kv, nk):
        n = nk * T

        keys = kvw[half, 0:nk, kv, 0].reshape(n, D)
        kt[:, 0:n] = keys.T
        dv_acc[0:n] = jnp.zeros((n, D), F32)

        def quad_step(i, carry):
            quad = half * 4 + kv * 2 + i
            q4 = four_heads(q, quad)
            top = None
            for d in range(nk):
                s = nt(kvw[half, d, kv, 0], q4)
                if d == 0:
                    s = s + bias[...]
                s_buf[d * T : (d + 1) * T] = s
                m = jnp.max(s, axis=0, keepdims=True)
                top = m if top is None else jnp.maximum(top, m)
            g4 = four_heads(g, quad)
            for d in range(nk):
                dp_buf[d * T : (d + 1) * T] = nt(kvw[half, d, kv, 1], g4)

            def exp_step(j, sums):
                rows = pl.ds(pl.multiple_of(j * CHUNK, CHUNK), CHUNK)
                e = jnp.exp2((s_buf[rows] - top) * exp2_scale)
                s_buf[rows] = e
                return (
                    sums[0] + jnp.sum(e.reshape(CHUNK // 8, 8, LANES), axis=0),
                    sums[1] + jnp.sum((e * dp_buf[rows]).reshape(CHUNK // 8, 8, LANES), axis=0),
                )

            zero = jnp.zeros((8, LANES), F32)
            total, weighted = lax.fori_loop(0, n // CHUNK, exp_step, (zero, zero), unroll=True)
            inv = 1.0 / jnp.sum(total, axis=0, keepdims=True)
            delta = jnp.sum(weighted, axis=0, keepdims=True) * inv

            def grad_step(j, carry):
                rows = pl.ds(pl.multiple_of(j * CHUNK, CHUNK), CHUNK)
                probs = s_buf[rows] * inv
                pb_buf[rows] = probs.astype(BF16)
                ds_buf[rows] = (probs * (dp_buf[rows] - delta)).astype(BF16)
                return carry

            lax.fori_loop(0, n // CHUNK, grad_step, 0, unroll=True)
            dv_acc[0:n] += nn(pb_buf[0:n], g4)
            gq[quad] = (nn(kt[:, 0:n], ds_buf[0:n]) * scale).astype(BF16)
            return carry

        lax.fori_loop(0, 2, quad_step, 0)
        dv_own[half, kv] = dv_acc[0:T]
        for d in range(1, nk):
            dv_snd[half, d - 1, kv] = dv_acc[d * T : (d + 1) * T].astype(BF16)
            dv_copy(half, d, kv).start()

    def dv_copy(half, d, kv):
        return remote(
            dv_snd.at[half, d - 1, kv],
            dv_rcv.at[half, d - 1, kv],
            dv_ssem.at[half, d - 1, kv],
            dv_rsem.at[half, d - 1, kv],
            lax.rem(c + CTX - d, CTX),
            p,
        )

    def hidden_layers():
        for copy in dw_loads:
            copy.wait()
        x_load.wait()

        def hidden_step(i, acc):
            cols = pl.ds(pl.multiple_of(i * 1024, 1024), 1024)
            return acc + nt(dw[:, cols], x[:, cols])

        hidden = lax.fori_loop(0, 8, hidden_step, jnp.zeros((32, T), F32))
        hid[...] = jnp.zeros_like(hid)
        hid[:, 0:T] = hidden.astype(BF16).astype(F32)
        ht4[...] = jnp.zeros_like(ht4)
        padded = hid[0:16, :]
        turned = pltpu.roll(padded, 64, 1)
        ht4[0:16, 0:256] = padded.astype(BF16)
        ht4[16:32, 128:384] = turned.astype(BF16)
        ht4[32:48, 384:640] = padded.astype(BF16)
        ht4[48:64, 512:768] = turned.astype(BF16)

    @pl.when(parity == 0)
    def _():
        def first_step(kv, carry):
            attend(first_half, kv, 1)

            @pl.when(kv == 0)
            def _():
                kv_arrived(second_half, 2, 0)
                kv_copy(second_half, 2, 0).start()
                kv_copy(second_half, 0, 1).start()
                kv_arrived(second_half, 1, 1)
                kv_copy(second_half, 1, 1).start()

            return carry

        lax.fori_loop(0, 2, first_step, 0)
        kv_arrived(second_half, 2, 1)
        kv_copy(second_half, 2, 1).start()
        hidden_layers()

        def second_step(kv, carry):
            attend(second_half, kv, 3)
            pl.when(kv == 0)(w_round_1)
            return carry

        lax.fori_loop(0, 2, second_step, 0)
        w_round_2()

    @pl.when(parity == 1)
    def _():
        def first_step(kv, carry):
            kv_arrived(first_half, 1, kv)
            kv_copy(first_half, 1, kv).start()
            attend(first_half, kv, 2)
            return carry

        lax.fori_loop(0, 2, first_step, 0)
        hidden_layers()

        def second_step(kv, carry):
            for slot in (1, 2, 3):
                kv_arrived(second_half, slot, kv)
            pl.when(kv == 0)(w_round_1)
            pl.when(kv == 1)(w_round_2)
            attend(second_half, kv, 4)
            return carry

        lax.fori_loop(0, 2, second_step, 0)

    with jax.named_scope("query_terms"):
        for copy in up_loads:
            copy.wait()
        flat_gq = gq[...].reshape(QUADS * D, LANES)
        up4 = jnp.concatenate(
            [
                jnp.concatenate(
                    [upq[:, (4 * i + j) * D : (4 * i + j + 1) * D] for i in range(QUADS)], axis=1
                )
                for j in range(4)
            ],
            axis=0,
        )
        r = nn(up4, flat_gq)
        code_q = (
            r[0:16, 0:256]
            + pltpu.roll(r[16:32, 128:384], 192, 1)
            + r[32:48, 384:640]
            + pltpu.roll(r[48:64, 512:768], 192, 1)
        )
        codes[...] = jnp.zeros_like(codes)
        codes[0:16, :] = code_q
        code_qt = codes[0:16, 0:T].astype(BF16)
        up_terms = nt(ht4[...], flat_gq)
        for i in range(DP):
            lo = 32 * (i % 2)
            col = D * (i // 2)
            term_q[i, :, 512:640] = up_terms[lo : lo + 16, col : col + D].astype(BF16)
            term_q[i, :, 640:768] = up_terms[lo + 16 : lo + 32, col : col + D].astype(BF16)

    def down_terms(term, code):
        def step(i, carry):
            cols = pl.ds(pl.multiple_of(i * SHARD, SHARD), SHARD)
            term[i, :, 0:SHARD] = nn(code, x[:, cols]).astype(BF16)
            return carry

        lax.fori_loop(0, DP, step, 0, unroll=4)

    def term_copy(which, off):
        target = lax.rem(p + off, DP)
        term, rcv = ((term_q, rcv_q), (term_v, rcv_v))[which]
        return remote(
            term.at[target],
            rcv.at[off],
            t_ssem.at[which, off],
            t_rsem.at[which, off],
            c,
            target,
        )

    def each(fn):
        def step(off, carry):
            fn(off)
            return carry

        lax.fori_loop(1, 16, step, 0, unroll=True)

    with jax.named_scope("query_down"):
        down_terms(term_q, code_qt)
        each(lambda off: term_copy(0, off).start())
        rcv_q[0] = term_q[p]

    with jax.named_scope("w_round_3"):
        w_arrived(7, 8, 9, 10)
        w_start(17, 18)

    with jax.named_scope("value_gradient"):
        for half in range(2):
            for d in range(1, 4):

                @pl.when(lags[half] + d <= 3)
                def _(half=half, d=d):
                    for kv in range(2):
                        dv_copy(half, d, kv).wait_recv()
                        dv_own[half, kv] += dv_rcv[half, d - 1, kv].astype(F32)

            for kv in range(2):
                col = (half * 2 + kv) * D
                gv[:, col : col + D] = dv_own[half, kv].astype(BF16)

        code_vt = nt(upv[...], gv[...])
        codes[16:32, 0:T] = code_vt
        code_vt = code_vt.astype(BF16)
        hidden_v = hid[16:32, 0:T].astype(BF16)
        up_v_terms = nn(hidden_v, gv[...])
        for i in range(DP):
            col = D * (i // 4)
            term_v[i, :, 512:640] = up_v_terms[:, col : col + D].astype(BF16)
        down_terms(term_v, code_vt)
        each(lambda off: term_copy(1, off).start())
        rcv_v[0] = term_v[p]

    with jax.named_scope("w_round_4"):
        w_arrived(11, 12)
        w_start(19)

    def input_gradient():
        w_load.wait()
        w_arrived(4, *range(13, 20))
        code = (ADAPTER_SCALE * codes[...].astype(BF16).astype(F32)).T
        code = code[0:T, :].astype(BF16)

        def step(i, carry):
            cols = pl.ds(pl.multiple_of(i * SHARD, SHARD), SHARD)
            dx[:, cols] = (nt(gv[...], w[i]) + nn(code, dw[:, cols])).astype(BF16)
            return carry

        lax.fori_loop(0, DP, step, 0, unroll=2)

    with jax.named_scope("sum_dp"):
        each(lambda off: term_copy(0, off).wait_recv())
        sum_q = jnp.sum(rcv_q[...].astype(F32), axis=0)
        rs_src[...] = jnp.zeros_like(rs_src)
        for j in range(6):
            rs_src[:, j, :] = sum_q[:, j * D : (j + 1) * D]
        each(lambda off: term_copy(1, off).wait_recv())
        sum_v = jnp.sum(rcv_v[...].astype(F32), axis=0)
        for j in range(5):
            rs_src[:, 6 + j, :] = sum_v[:, j * D : (j + 1) * D]

    def row_copy(off):
        target = lax.rem(c + off, CTX)
        return remote(
            rs_src.at[target], rs_rcv.at[off], r_ssem.at[0, off], r_rsem.at[0, off], target, p
        )

    def sum_copy(off):
        target = lax.rem(c + off, CTX)
        return remote(ag.at[c], ag.at[c], r_ssem.at[1, off], r_rsem.at[1, off], target, p)

    def sum_arrived(off):
        src = lax.rem(c + CTX - off, CTX)
        remote(ag.at[src], ag.at[src], r_ssem.at[1, off], r_rsem.at[1, off], src, p).wait_recv()

    for off in FAR_FIRST:
        row_copy(off).start()
    rs_rcv[0] = rs_src[c]

    z = lax.rem(c, 8)
    early = (z <= 2) | (z >= 6)
    with jax.named_scope("dx_early"):
        pl.when(early)(input_gradient)
    with jax.named_scope("sum_ctx"):
        each(lambda off: row_copy(off).wait_recv())
        gradient_scale = ADAPTER_SCALE / math.sqrt(DP * CTX * T)
        ag[c] = jnp.sum(rs_rcv[...], axis=0) * gradient_scale
        for off in FAR_FIRST:
            sum_copy(off).start()
    with jax.named_scope("dx_late"):
        pl.when(jnp.logical_not(early))(input_gradient)
    with jax.named_scope("outputs"):
        each(sum_arrived)
        ag_out[...] = ag[...]

    with jax.named_scope("drain"):
        for kv in range(2):
            kv_copy(first_half, 0, kv).wait_send()

        @pl.when(parity == 0)
        def _():
            for slot in range(3):
                for kv in range(2):
                    kv_copy(second_half, slot, kv).wait_send()

        @pl.when(parity == 1)
        def _():
            for kv in range(2):
                kv_copy(first_half, 1, kv).wait_send()

        for half in range(2):
            for d in range(1, 4):

                @pl.when(lags[half] >= d)
                def _(half=half, d=d):
                    for kv in range(2):
                        dv_copy(half, d, kv).wait_send()

        for number in range(20):
            w_copy(number).wait_send()

        def sent(off):
            term_copy(0, off).wait_send()
            term_copy(1, off).wait_send()
            row_copy(off).wait_send()
            sum_copy(off).wait_send()

        each(sent)


def place(sums, dx, down_q_out, up_q_out, down_v_out, up_v_out, dx_out, wide, narrow, sem):
    p = lax.axis_index("dp")
    copies = [pltpu.make_async_copy(dx, dx_out.at[0], sem.at[0])]
    copies[0].start()
    for j in range(11):
        wide[:, j * D : (j + 1) * D] = sums[:, j, :]
    piece = sums[:, 10, :]
    for j in range(4):

        @pl.when(lax.rem(p, 4) == j)
        def _(j=j):
            narrow[...] = piece[:, 32 * j : 32 * (j + 1)]

    for src, dst in (
        (wide.at[:, 0:512], down_q_out),
        (wide.at[:, 512:768], up_q_out),
        (wide.at[:, 768:1280], down_v_out),
        (narrow, up_v_out),
    ):
        copies.append(pltpu.make_async_copy(src, dst, sem.at[len(copies)]))
        copies[-1].start()
    for copy in copies:
        copy.wait()


def deliver(sums, dx):
    return pl.pallas_call(
        place,
        out_shape=(
            jax.ShapeDtypeStruct((16, SHARD), F32),
            jax.ShapeDtypeStruct((16, DQ // DP), F32),
            jax.ShapeDtypeStruct((16, SHARD), F32),
            jax.ShapeDtypeStruct((16, DKV // DP), F32),
            jax.ShapeDtypeStruct((1, T, WIDTH), BF16),
        ),
        in_specs=[pl.BlockSpec(memory_space=pltpu.VMEM)] * 2,
        out_specs=[pl.BlockSpec(memory_space=pl.ANY)] * 5,
        scratch_shapes=[
            pltpu.VMEM((16, 11 * D), F32),
            pltpu.VMEM((16, DKV // DP), F32),
            pltpu.SemaphoreType.DMA((5,)),
        ],
        compiler_params=pltpu.CompilerParams(vmem_limit_bytes=16 * 1024 * 1024),
    )(
        pltpu.with_memory_space_constraint(sums, pltpu.VMEM),
        pltpu.with_memory_space_constraint(dx, pltpu.VMEM),
    )


def on_device(
    inputs,
    query_saved,
    key_saved,
    value_saved,
    grad_out,
    value_weight,
    query_down_weight,
    up_q,
    value_down_weight,
    up_v,
):
    sums, dx = pl.pallas_call(
        kernel,
        out_shape=(
            pltpu.VMEM((CTX, 16, D), F32),
            pltpu.VMEM((T, WIDTH), BF16),
        ),
        in_specs=[pl.BlockSpec(memory_space=pl.ANY)] * 10,
        out_specs=[pl.BlockSpec(memory_space=pltpu.VMEM)] * 2,
        scratch_shapes=[
            pltpu.VMEM((T, WIDTH), BF16),
            pltpu.VMEM((T, DQ), BF16),
            pltpu.VMEM((T, DQ), BF16),
            pltpu.VMEM((2, 4, 2, 2, T, D), BF16),
            pltpu.VMEM((DP, SHARD, DKV), BF16),
            pltpu.VMEM((32, WIDTH), BF16),
            pltpu.VMEM((16, DQ), BF16),
            pltpu.VMEM((16, DKV), BF16),
            pltpu.VMEM((T, LANES), F32),
            pltpu.VMEM((4 * T, LANES), F32),
            pltpu.VMEM((4 * T, LANES), F32),
            pltpu.VMEM((4 * T, LANES), BF16),
            pltpu.VMEM((4 * T, LANES), BF16),
            pltpu.VMEM((D, 4 * T), BF16),
            pltpu.VMEM((4 * T, D), F32),
            pltpu.VMEM((2, 2, T, D), F32),
            pltpu.VMEM((2, 3, 2, T, D), BF16),
            pltpu.VMEM((2, 3, 2, T, D), BF16),
            pltpu.VMEM((QUADS, D, LANES), BF16),
            pltpu.VMEM((T, DKV), BF16),
            pltpu.VMEM((32, 256), F32),
            pltpu.VMEM((64, LANES), BF16),
            pltpu.VMEM((32, 256), F32),
            pltpu.VMEM((DP, 16, 768), BF16),
            pltpu.VMEM((DP, 16, 640), BF16),
            pltpu.VMEM((DP, 16, 768), BF16),
            pltpu.VMEM((DP, 16, 640), BF16),
            pltpu.VMEM((CTX, 16, D), F32),
            pltpu.VMEM((CTX, 16, D), F32),
            pltpu.VMEM((CTX, 16, D), F32),
            pltpu.SemaphoreType.DMA((16,)),
            pltpu.SemaphoreType.DMA((2, 4, 2)),
            pltpu.SemaphoreType.DMA((2, 4, 2)),
            pltpu.SemaphoreType.DMA((20,)),
            pltpu.SemaphoreType.DMA((20,)),
            pltpu.SemaphoreType.DMA((2, 3, 2)),
            pltpu.SemaphoreType.DMA((2, 3, 2)),
            pltpu.SemaphoreType.DMA((2, 16)),
            pltpu.SemaphoreType.DMA((2, 16)),
            pltpu.SemaphoreType.DMA((2, 16)),
            pltpu.SemaphoreType.DMA((2, 16)),
        ],
        compiler_params=pltpu.CompilerParams(
            collective_id=0, has_side_effects=True, vmem_limit_bytes=44 * 1024 * 1024
        ),
    )(
        *(
            pltpu.with_memory_space_constraint(operand, pltpu.HBM)
            for operand in (
                inputs[0],
                query_saved[0],
                key_saved[0],
                value_saved[0],
                grad_out[0],
                value_weight,
                query_down_weight,
                up_q,
                value_down_weight,
                up_v,
            )
        )
    )
    return deliver(sums, dx)


def solution(mesh):
    in_specs = (
        P("dp", "ctx", None),
        P("dp", "ctx", None),
        P("dp", "ctx", None),
        P("dp", "ctx", None),
        P("dp", "ctx", None),
        P("dp", None),
        P(),
        P(),
        P(),
        P(),
    )
    out_specs = (P(None, "dp"), P(None, "dp"), P(None, "dp"), P(None, "dp"), P("dp", "ctx", None))
    return jax.shard_map(
        on_device, mesh=mesh, in_specs=in_specs, out_specs=out_specs, check_vma=False
    )
```

```python
import functools
import math

import jax
import jax.numpy as jnp
from jax import lax
from jax.experimental import pallas as pl
from jax.experimental.pallas import tpu as pltpu
from jax.sharding import PartitionSpec as P

MESH = pl.DeviceIdType.MESH
F32 = jnp.float32
BF16 = jnp.bfloat16

CTX = 16
DP = 16
T = 192
D = 128
LANES = 4 * T
QUADS = 8
WIDTH = 8192
SHARD = WIDTH // DP
DQ = 4096
DKV = 512
ADAPTER_SCALE = 2.0
CHUNK = 32
FAR_FIRST = (4, 12, 3, 5, 11, 13, 2, 6, 10, 14, 1, 7, 9, 15, 8)


def nt(a, b):
    return lax.dot_general(a, b, (((1,), (1,)), ((), ())), preferred_element_type=F32)


def nn(a, b):
    return jnp.dot(a, b, preferred_element_type=F32)


def kernel(
    x_hbm,
    q_hbm,
    k_hbm,
    v_hbm,
    g_hbm,
    w_hbm,
    qdw_hbm,
    upq_hbm,
    vdw_hbm,
    upv_hbm,
    ag_out,
    dx,
    x,
    q,
    g,
    kvw,
    w,
    dw,
    upq,
    upv,
    bias,
    s_buf,
    dp_buf,
    pb_buf,
    ds_buf,
    kt,
    dv_acc,
    dv_own,
    dv_snd,
    dv_rcv,
    gq,
    gv,
    hid,
    ht4,
    codes,
    term_q,
    term_v,
    rcv_q,
    rcv_v,
    rs_src,
    rs_rcv,
    ag,
    loc_sem,
    kv_ssem,
    kv_rsem,
    w_ssem,
    w_rsem,
    dv_ssem,
    dv_rsem,
    t_ssem,
    t_rsem,
    r_ssem,
    r_rsem,
):
    c = lax.axis_index("ctx")
    p = lax.axis_index("dp")
    right = lax.rem(c + 1, CTX)
    scale = 1.0 / math.sqrt(D)
    exp2_scale = scale * math.log2(math.e)

    def remote(src, dst, ssem, rsem, ctx, dp):
        return pltpu.make_async_remote_copy(
            src_ref=src,
            dst_ref=dst,
            send_sem=ssem,
            recv_sem=rsem,
            device_id=(ctx, dp),
            device_id_type=MESH,
        )

    loads = []

    def load(src, dst):
        copy = pltpu.make_async_copy(src, dst, loc_sem.at[len(loads)])
        copy.start()
        loads.append(copy)
        return copy

    kv_loads = []
    for half in range(2):
        for which, ref in ((0, k_hbm), (1, v_hbm)):
            for head in range(2):
                col = (half * 2 + head) * D
                kv_loads.append(load(ref.at[:, col : col + D], kvw.at[half, 0, head, which]))
    with jax.named_scope("greet"):
        barrier = pltpu.get_barrier_semaphore()

        def greet(off, carry):
            pl.semaphore_signal(
                barrier, inc=1, device_id=(lax.rem(c + off, CTX), p), device_id_type=MESH
            )
            pl.semaphore_signal(
                barrier, inc=1, device_id=(c, lax.rem(p + off, DP)), device_id_type=MESH
            )
            return carry

        lax.fori_loop(1, 16, greet, 0, unroll=True)
        pl.semaphore_signal(
            barrier,
            inc=1,
            device_id=(lax.rem(c + 8, CTX), lax.rem(p + 8, DP)),
            device_id_type=MESH,
        )
        q_load = load(q_hbm, q)
        g_load = load(g_hbm, g)
        dw_loads = [load(qdw_hbm, dw.at[0:16]), load(vdw_hbm, dw.at[16:32])]
        x_load = load(x_hbm, x)
        up_loads = [load(upq_hbm, upq), load(upv_hbm, upv)]
        w_load = load(w_hbm, w.at[p])
        pl.semaphore_wait(barrier, 31)

    lags = (lax.rem(c, 4), lax.rem(c + 2, 4))
    parity = lax.rem(c, 2)
    first_half = lax.rem(c, 4) // 2
    second_half = 1 - first_half

    def kv_copy(half, slot, kv):
        return remote(
            kvw.at[half, slot, kv],
            kvw.at[half, slot + 1, kv],
            kv_ssem.at[half, slot, kv],
            kv_rsem.at[half, slot + 1, kv],
            right,
            p,
        )

    def kv_arrived(half, slot, kv):
        remote(
            kvw.at[half, slot, kv],
            kvw.at[half, slot, kv],
            kv_ssem.at[half, slot, kv],
            kv_rsem.at[half, slot, kv],
            right,
            p,
        ).wait_recv()

    with jax.named_scope("kv_send"):
        for copy in kv_loads:
            copy.wait()
        for kv in range(2):
            kv_copy(first_half, 0, kv).start()

        @pl.when(parity == 0)
        def _():
            kv_copy(second_half, 0, 0).start()

    core = lax.rem(p, 2)
    px = lax.rem(p // 2, 4)
    py = p // 8

    def at(dy, dx_, dc):
        yy = lax.rem(py + dy, 2)
        xx = lax.rem(px + dx_ + 4, 4)
        cc = lax.rem(core + dc, 2)
        return yy * 8 + xx * 2 + cc

    x_up, x_dn, y_nb, sib = at(0, 1, 0), at(0, -1, 0), at(1, 0, 0), at(0, 0, 1)
    far = lax.rem(c + 8, CTX)
    rows = SHARD // 2
    own, up, dn, opp = p, x_up, x_dn, at(0, 2, 0)
    y_own, y_up, y_dn, y_opp = at(1, 0, 0), at(1, 1, 0), at(1, -1, 0), at(1, 2, 0)
    w_plan = [
        (own, dn, 2, c, x_up),
        (own, up, 2, c, x_dn),
        (own, y_own, 0, c, y_nb),
        (own, y_own, 1, far, y_nb),
        (own, sib, 2, c, sib),
        (up, opp, 0, c, x_dn),
        (dn, opp, 1, c, x_up),
        (up, y_up, 0, c, y_nb),
        (dn, y_dn, 0, far, y_nb),
        (y_own, y_up, 1, c, x_dn),
        (y_own, y_dn, 1, c, x_up),
        (opp, y_opp, 0, c, y_nb),
        (opp, y_opp, 1, far, y_nb),
        (dn, at(0, -1, 1), 2, c, sib),
        (up, at(0, 1, 1), 2, c, sib),
        (y_own, at(1, 0, 1), 2, c, sib),
        (opp, at(0, 2, 1), 2, c, sib),
        (y_up, at(1, 1, 1), 2, c, sib),
        (y_dn, at(1, -1, 1), 2, c, sib),
        (y_opp, at(1, 2, 1), 2, c, sib),
    ]

    def w_part(shard, part):
        return w.at[shard] if part == 2 else w.at[shard, part * rows : (part + 1) * rows]

    def w_copy(number):
        shard, _, part, ctx, target = w_plan[number]
        block = w_part(shard, part)
        src = block
        if number < 5:
            src = w_hbm if part == 2 else w_hbm.at[part * rows : (part + 1) * rows]
        return remote(src, block, w_ssem.at[number], w_rsem.at[number], ctx, target)

    def w_arrived(*numbers):
        for number in numbers:
            _, shard, part, ctx, target = w_plan[number]
            block = w_part(shard, part)
            remote(
                block, block, w_ssem.at[number], w_rsem.at[number], ctx, target
            ).wait_recv()

    def w_start(*numbers):
        for number in numbers:
            w_copy(number).start()

    def w_round_1():
        with jax.named_scope("w_round_1"):
            w_arrived(0, 1, 2, 3)
            w_start(5, 6, 7, 8, 9, 10, 13, 14, 15)

    def w_round_2():
        with jax.named_scope("w_round_2"):
            w_arrived(5, 6)
            w_start(11, 12, 16)

    w_start(2, 3, 0, 1, 4)

    with jax.named_scope("bias"):
        row = lax.broadcasted_iota(jnp.int32, (T, LANES), 0)
        lane = lax.broadcasted_iota(jnp.int32, (T, LANES), 1)
        turn = (
            (lane >= T).astype(jnp.int32)
            + (lane >= 2 * T).astype(jnp.int32)
            + (lane >= 3 * T).astype(jnp.int32)
        )
        bias[...] = jnp.where(row <= lane - turn * T, 0.0, -jnp.inf).astype(F32)

    @pl.when(parity == 0)
    def _():
        kv_arrived(second_half, 1, 0)
        kv_copy(second_half, 1, 0).start()

    q_load.wait()
    g_load.wait()

    def four_heads(ref, quad):
        block = ref[:, pl.ds(pl.multiple_of(quad * 512, 512), 512)]
        return jnp.concatenate([block[:, i * D : (i + 1) * D] for i in range(4)], axis=0)

    def attend(half, kv, nk):
        n = nk * T

        keys = kvw[half, 0:nk, kv, 0].reshape(n, D)
        kt[:, 0:n] = keys.T
        dv_acc[0:n] = jnp.zeros((n, D), F32)

        def quad_step(i, carry):
            quad = half * 4 + kv * 2 + i
            q4 = four_heads(q, quad)
            top = None
            for d in range(nk):
                s = nt(kvw[half, d, kv, 0], q4)
                if d == 0:
                    s = s + bias[...]
                s_buf[d * T : (d + 1) * T] = s
                m = jnp.max(s, axis=0, keepdims=True)
                top = m if top is None else jnp.maximum(top, m)
            g4 = four_heads(g, quad)
            for d in range(nk):
                dp_buf[d * T : (d + 1) * T] = nt(kvw[half, d, kv, 1], g4)

            def exp_step(j, sums):
                rows = pl.ds(pl.multiple_of(j * CHUNK, CHUNK), CHUNK)
                e = jnp.exp2((s_buf[rows] - top) * exp2_scale)
                s_buf[rows] = e
                return (
                    sums[0] + jnp.sum(e.reshape(CHUNK // 8, 8, LANES), axis=0),
                    sums[1] + jnp.sum((e * dp_buf[rows]).reshape(CHUNK // 8, 8, LANES), axis=0),
                )

            zero = jnp.zeros((8, LANES), F32)
            total, weighted = lax.fori_loop(0, n // CHUNK, exp_step, (zero, zero), unroll=True)
            inv = 1.0 / jnp.sum(total, axis=0, keepdims=True)
            delta = jnp.sum(weighted, axis=0, keepdims=True) * inv

            def grad_step(j, carry):
                rows = pl.ds(pl.multiple_of(j * CHUNK, CHUNK), CHUNK)
                probs = s_buf[rows] * inv
                pb_buf[rows] = probs.astype(BF16)
                ds_buf[rows] = (probs * (dp_buf[rows] - delta)).astype(BF16)
                return carry

            lax.fori_loop(0, n // CHUNK, grad_step, 0, unroll=True)
            dv_acc[0:n] += nn(pb_buf[0:n], g4)
            gq[quad] = (nn(kt[:, 0:n], ds_buf[0:n]) * scale).astype(BF16)
            return carry

        lax.fori_loop(0, 2, quad_step, 0)
        dv_own[half, kv] = dv_acc[0:T]
        for d in range(1, nk):
            dv_snd[half, d - 1, kv] = dv_acc[d * T : (d + 1) * T].astype(BF16)
            dv_copy(half, d, kv).start()

    def dv_copy(half, d, kv):
        return remote(
            dv_snd.at[half, d - 1, kv],
            dv_rcv.at[half, d - 1, kv],
            dv_ssem.at[half, d - 1, kv],
            dv_rsem.at[half, d - 1, kv],
            lax.rem(c + CTX - d, CTX),
            p,
        )

    def hidden_layers():
        for copy in dw_loads:
            copy.wait()
        x_load.wait()

        def hidden_step(i, acc):
            cols = pl.ds(pl.multiple_of(i * 1024, 1024), 1024)
            return acc + nt(dw[:, cols], x[:, cols])

        hidden = lax.fori_loop(0, 8, hidden_step, jnp.zeros((32, T), F32))
        hid[...] = jnp.zeros_like(hid)
        hid[:, 0:T] = hidden.astype(BF16).astype(F32)
        ht4[...] = jnp.zeros_like(ht4)
        padded = hid[0:16, :]
        turned = pltpu.roll(padded, 64, 1)
        ht4[0:16, 0:256] = padded.astype(BF16)
        ht4[16:32, 128:384] = turned.astype(BF16)
        ht4[32:48, 384:640] = padded.astype(BF16)
        ht4[48:64, 512:768] = turned.astype(BF16)

    @pl.when(parity == 0)
    def _():
        def first_step(kv, carry):
            attend(first_half, kv, 1)

            @pl.when(kv == 0)
            def _():
                kv_arrived(second_half, 2, 0)
                kv_copy(second_half, 2, 0).start()
                kv_copy(second_half, 0, 1).start()
                kv_arrived(second_half, 1, 1)
                kv_copy(second_half, 1, 1).start()

            return carry

        lax.fori_loop(0, 2, first_step, 0)
        kv_arrived(second_half, 2, 1)
        kv_copy(second_half, 2, 1).start()
        hidden_layers()

        def second_step(kv, carry):
            attend(second_half, kv, 3)
            pl.when(kv == 0)(w_round_1)
            return carry

        lax.fori_loop(0, 2, second_step, 0)
        w_round_2()

    @pl.when(parity == 1)
    def _():
        def first_step(kv, carry):
            kv_arrived(first_half, 1, kv)
            kv_copy(first_half, 1, kv).start()
            attend(first_half, kv, 2)
            return carry

        lax.fori_loop(0, 2, first_step, 0)
        hidden_layers()

        def second_step(kv, carry):
            for slot in (1, 2, 3):
                kv_arrived(second_half, slot, kv)
            pl.when(kv == 0)(w_round_1)
            pl.when(kv == 1)(w_round_2)
            attend(second_half, kv, 4)
            return carry

        lax.fori_loop(0, 2, second_step, 0)

    with jax.named_scope("query_terms"):
        for copy in up_loads:
            copy.wait()
        flat_gq = gq[...].reshape(QUADS * D, LANES)
        up4 = jnp.concatenate(
            [
                jnp.concatenate(
                    [upq[:, (4 * i + j) * D : (4 * i + j + 1) * D] for i in range(QUADS)], axis=1
                )
                for j in range(4)
            ],
            axis=0,
        )
        r = nn(up4, flat_gq)
        code_q = (
            r[0:16, 0:256]
            + pltpu.roll(r[16:32, 128:384], 192, 1)
            + r[32:48, 384:640]
            + pltpu.roll(r[48:64, 512:768], 192, 1)
        )
        codes[...] = jnp.zeros_like(codes)
        codes[0:16, :] = code_q
        code_qt = codes[0:16, 0:T].astype(BF16)
        up_terms = nt(ht4[...], flat_gq)
        for i in range(DP):
            lo = 32 * (i % 2)
            col = D * (i // 2)
            term_q[i, :, 512:640] = up_terms[lo : lo + 16, col : col + D].astype(BF16)
            term_q[i, :, 640:768] = up_terms[lo + 16 : lo + 32, col : col + D].astype(BF16)

    def down_terms(term, code):
        def step(i, carry):
            cols = pl.ds(pl.multiple_of(i * SHARD, SHARD), SHARD)
            term[i, :, 0:SHARD] = nn(code, x[:, cols]).astype(BF16)
            return carry

        lax.fori_loop(0, DP, step, 0, unroll=4)

    def term_copy(which, off):
        target = lax.rem(p + off, DP)
        term, rcv = ((term_q, rcv_q), (term_v, rcv_v))[which]
        return remote(
            term.at[target],
            rcv.at[off],
            t_ssem.at[which, off],
            t_rsem.at[which, off],
            c,
            target,
        )

    def each(fn):
        def step(off, carry):
            fn(off)
            return carry

        lax.fori_loop(1, 16, step, 0, unroll=True)

    with jax.named_scope("query_down"):
        down_terms(term_q, code_qt)
        each(lambda off: term_copy(0, off).start())
        rcv_q[0] = term_q[p]

    with jax.named_scope("value_gradient"):
        for half in range(2):
            for d in range(1, 4):

                @pl.when(lags[half] + d <= 3)
                def _(half=half, d=d):
                    for kv in range(2):
                        dv_copy(half, d, kv).wait_recv()
                        dv_own[half, kv] += dv_rcv[half, d - 1, kv].astype(F32)

            for kv in range(2):
                col = (half * 2 + kv) * D
                gv[:, col : col + D] = dv_own[half, kv].astype(BF16)

        code_vt = nt(upv[...], gv[...])
        codes[16:32, 0:T] = code_vt
        code_vt = code_vt.astype(BF16)
        hidden_v = hid[16:32, 0:T].astype(BF16)
        up_v_terms = nn(hidden_v, gv[...])
        for i in range(DP):
            col = D * (i // 4)
            term_v[i, :, 512:640] = up_v_terms[:, col : col + D].astype(BF16)
        down_terms(term_v, code_vt)
        each(lambda off: term_copy(1, off).start())
        rcv_v[0] = term_v[p]

    def input_gradient():
        w_load.wait()
        w_arrived(4, *range(13, 20))
        code = (ADAPTER_SCALE * codes[...].astype(BF16).astype(F32)).T
        code = code[0:T, :].astype(BF16)

        def step(i, carry):
            cols = pl.ds(pl.multiple_of(i * SHARD, SHARD), SHARD)
            dx[:, cols] = (nt(gv[...], w[i]) + nn(code, dw[:, cols])).astype(BF16)
            return carry

        lax.fori_loop(0, DP, step, 0, unroll=2)

    with jax.named_scope("sum_dp"):
        each(lambda off: term_copy(0, off).wait_recv())
        sum_q = jnp.sum(rcv_q[...].astype(F32), axis=0)
        rs_src[...] = jnp.zeros_like(rs_src)
        for j in range(6):
            rs_src[:, j, :] = sum_q[:, j * D : (j + 1) * D]
        each(lambda off: term_copy(1, off).wait_recv())
        sum_v = jnp.sum(rcv_v[...].astype(F32), axis=0)
        for j in range(5):
            rs_src[:, 6 + j, :] = sum_v[:, j * D : (j + 1) * D]

    def row_copy(off):
        target = lax.rem(c + off, CTX)
        return remote(
            rs_src.at[target], rs_rcv.at[off], r_ssem.at[0, off], r_rsem.at[0, off], target, p
        )

    def sum_copy(off):
        target = lax.rem(c + off, CTX)
        return remote(ag.at[c], ag.at[c], r_ssem.at[1, off], r_rsem.at[1, off], target, p)

    def sum_arrived(off):
        src = lax.rem(c + CTX - off, CTX)
        remote(ag.at[src], ag.at[src], r_ssem.at[1, off], r_rsem.at[1, off], src, p).wait_recv()

    for off in FAR_FIRST:
        row_copy(off).start()
    rs_rcv[0] = rs_src[c]

    with jax.named_scope("w_round_3"):
        w_arrived(7, 8, 9, 10)
        w_start(17, 18)

    with jax.named_scope("w_round_4"):
        w_arrived(11, 12)
        w_start(19)

    z = lax.rem(c, 8)
    early = (z <= 2) | (z >= 6)
    with jax.named_scope("dx_early"):
        pl.when(early)(input_gradient)
    with jax.named_scope("sum_ctx"):
        each(lambda off: row_copy(off).wait_recv())
        gradient_scale = ADAPTER_SCALE / math.sqrt(DP * CTX * T)
        ag[c] = jnp.sum(rs_rcv[...], axis=0) * gradient_scale
        for off in FAR_FIRST:
            sum_copy(off).start()
    with jax.named_scope("dx_late"):
        pl.when(jnp.logical_not(early))(input_gradient)
    with jax.named_scope("outputs"):
        each(sum_arrived)
        ag_out[...] = ag[...]

    with jax.named_scope("drain"):
        for kv in range(2):
            kv_copy(first_half, 0, kv).wait_send()

        @pl.when(parity == 0)
        def _():
            for slot in range(3):
                for kv in range(2):
                    kv_copy(second_half, slot, kv).wait_send()

        @pl.when(parity == 1)
        def _():
            for kv in range(2):
                kv_copy(first_half, 1, kv).wait_send()

        for half in range(2):
            for d in range(1, 4):

                @pl.when(lags[half] >= d)
                def _(half=half, d=d):
                    for kv in range(2):
                        dv_copy(half, d, kv).wait_send()

        for number in range(20):
            w_copy(number).wait_send()

        def sent(off):
            term_copy(0, off).wait_send()
            term_copy(1, off).wait_send()
            row_copy(off).wait_send()
            sum_copy(off).wait_send()

        each(sent)


def place(sums, dx, down_q_out, up_q_out, down_v_out, up_v_out, dx_out, wide, narrow, sem):
    p = lax.axis_index("dp")
    copies = [pltpu.make_async_copy(dx, dx_out.at[0], sem.at[0])]
    copies[0].start()
    for j in range(11):
        wide[:, j * D : (j + 1) * D] = sums[:, j, :]
    piece = sums[:, 10, :]
    for j in range(4):

        @pl.when(lax.rem(p, 4) == j)
        def _(j=j):
            narrow[...] = piece[:, 32 * j : 32 * (j + 1)]

    for src, dst in (
        (wide.at[:, 0:512], down_q_out),
        (wide.at[:, 512:768], up_q_out),
        (wide.at[:, 768:1280], down_v_out),
        (narrow, up_v_out),
    ):
        copies.append(pltpu.make_async_copy(src, dst, sem.at[len(copies)]))
        copies[-1].start()
    for copy in copies:
        copy.wait()


def deliver(sums, dx):
    return pl.pallas_call(
        place,
        out_shape=(
            jax.ShapeDtypeStruct((16, SHARD), F32),
            jax.ShapeDtypeStruct((16, DQ // DP), F32),
            jax.ShapeDtypeStruct((16, SHARD), F32),
            jax.ShapeDtypeStruct((16, DKV // DP), F32),
            jax.ShapeDtypeStruct((1, T, WIDTH), BF16),
        ),
        in_specs=[pl.BlockSpec(memory_space=pltpu.VMEM)] * 2,
        out_specs=[pl.BlockSpec(memory_space=pl.ANY)] * 5,
        scratch_shapes=[
            pltpu.VMEM((16, 11 * D), F32),
            pltpu.VMEM((16, DKV // DP), F32),
            pltpu.SemaphoreType.DMA((5,)),
        ],
        compiler_params=pltpu.CompilerParams(vmem_limit_bytes=16 * 1024 * 1024),
    )(
        pltpu.with_memory_space_constraint(sums, pltpu.VMEM),
        pltpu.with_memory_space_constraint(dx, pltpu.VMEM),
    )


def on_device(
    inputs,
    query_saved,
    key_saved,
    value_saved,
    grad_out,
    value_weight,
    query_down_weight,
    up_q,
    value_down_weight,
    up_v,
):
    sums, dx = pl.pallas_call(
        kernel,
        out_shape=(
            pltpu.VMEM((CTX, 16, D), F32),
            pltpu.VMEM((T, WIDTH), BF16),
        ),
        in_specs=[pl.BlockSpec(memory_space=pl.ANY)] * 10,
        out_specs=[pl.BlockSpec(memory_space=pltpu.VMEM)] * 2,
        scratch_shapes=[
            pltpu.VMEM((T, WIDTH), BF16),
            pltpu.VMEM((T, DQ), BF16),
            pltpu.VMEM((T, DQ), BF16),
            pltpu.VMEM((2, 4, 2, 2, T, D), BF16),
            pltpu.VMEM((DP, SHARD, DKV), BF16),
            pltpu.VMEM((32, WIDTH), BF16),
            pltpu.VMEM((16, DQ), BF16),
            pltpu.VMEM((16, DKV), BF16),
            pltpu.VMEM((T, LANES), F32),
            pltpu.VMEM((4 * T, LANES), F32),
            pltpu.VMEM((4 * T, LANES), F32),
            pltpu.VMEM((4 * T, LANES), BF16),
            pltpu.VMEM((4 * T, LANES), BF16),
            pltpu.VMEM((D, 4 * T), BF16),
            pltpu.VMEM((4 * T, D), F32),
            pltpu.VMEM((2, 2, T, D), F32),
            pltpu.VMEM((2, 3, 2, T, D), BF16),
            pltpu.VMEM((2, 3, 2, T, D), BF16),
            pltpu.VMEM((QUADS, D, LANES), BF16),
            pltpu.VMEM((T, DKV), BF16),
            pltpu.VMEM((32, 256), F32),
            pltpu.VMEM((64, LANES), BF16),
            pltpu.VMEM((32, 256), F32),
            pltpu.VMEM((DP, 16, 768), BF16),
            pltpu.VMEM((DP, 16, 640), BF16),
            pltpu.VMEM((DP, 16, 768), BF16),
            pltpu.VMEM((DP, 16, 640), BF16),
            pltpu.VMEM((CTX, 16, D), F32),
            pltpu.VMEM((CTX, 16, D), F32),
            pltpu.VMEM((CTX, 16, D), F32),
            pltpu.SemaphoreType.DMA((16,)),
            pltpu.SemaphoreType.DMA((2, 4, 2)),
            pltpu.SemaphoreType.DMA((2, 4, 2)),
            pltpu.SemaphoreType.DMA((20,)),
            pltpu.SemaphoreType.DMA((20,)),
            pltpu.SemaphoreType.DMA((2, 3, 2)),
            pltpu.SemaphoreType.DMA((2, 3, 2)),
            pltpu.SemaphoreType.DMA((2, 16)),
            pltpu.SemaphoreType.DMA((2, 16)),
            pltpu.SemaphoreType.DMA((2, 16)),
            pltpu.SemaphoreType.DMA((2, 16)),
        ],
        compiler_params=pltpu.CompilerParams(
            collective_id=0, has_side_effects=True, vmem_limit_bytes=44 * 1024 * 1024
        ),
    )(
        *(
            pltpu.with_memory_space_constraint(operand, pltpu.HBM)
            for operand in (
                inputs[0],
                query_saved[0],
                key_saved[0],
                value_saved[0],
                grad_out[0],
                value_weight,
                query_down_weight,
                up_q,
                value_down_weight,
                up_v,
            )
        )
    )
    return deliver(sums, dx)


def solution(mesh):
    in_specs = (
        P("dp", "ctx", None),
        P("dp", "ctx", None),
        P("dp", "ctx", None),
        P("dp", "ctx", None),
        P("dp", "ctx", None),
        P("dp", None),
        P(),
        P(),
        P(),
        P(),
    )
    out_specs = (P(None, "dp"), P(None, "dp"), P(None, "dp"), P(None, "dp"), P("dp", "ctx", None))
    return jax.shard_map(
        on_device, mesh=mesh, in_specs=in_specs, out_specs=out_specs, check_vma=False
    )
```
